256 devices in a mesh: freq: 4 (over y_hi, core), blk: 64 (over x, y_lo, z).
Axes of the slice: x: 4, y: 4 (y_hi: 2, y_lo: 2; y = y_hi * 2 + y_lo), z: 8, core: 2. Of those that a mesh axis runs over, the one named last changes fastest.
Arguments:
- panels: bfloat16 [8, 2, 8192, 8192], P('freq', None, 'blk'), parts along dimension 0, may hold values from -30 to 30
- test_matrix: bfloat16 [8192, 256], P('blk'), may hold values from -0.0625 to 0.0625
Outputs:
- projected: float32 [8192, 8, 256], P('blk', 'freq'), parts along dimension 1
The draws below stay inside these ranges and needn't reach their ends.
There are 4 independent parts, one for each index of `freq`. The reference program is written for one: setup_inputs(seed, part) draws one part's arguments, and reference() takes and returns one part's arrays. A program takes and returns all parts, laid end to end along the dimension named above; an argument that names none is the same for every part. Nothing has to cross between parts.
All inputs are finite; a program needn't handle non-finite values.
Results may differ from the reference program's by a relative error of at most 0.0017.
Values may be sent and summed in bfloat16 or wider, within the bound.
A program may use at most 128 MiB of HBM per device.

```python
import jax
import jax.numpy as jnp
from jax import lax

N = 8192
K = 256
SLICES = 2
ROWS = 8192


def draw_panels(key, part):
    key = jax.random.fold_in(key, 11)
    first_key, second_key, third_key = jax.random.split(key, 3)
    position = jnp.arange(ROWS, dtype=jnp.float32).reshape(1, 1, ROWS, 1) / ROWS
    jitter = jax.random.uniform(second_key, (SLICES, 1, ROWS, 1), jnp.float32)
    row_scale = 10.0 ** (0.5 * position + 0.5 * jitter)
    column_draw = jax.random.uniform(third_key, (SLICES, 1, 1, N), jnp.float32)
    values = jnp.clip(jax.random.normal(first_key, (SLICES, 2, ROWS, N), jnp.float32), -6.0, 6.0)
    column_scale = 10.0 ** column_draw
    return (0.05 * values * row_scale * column_scale).astype(jnp.bfloat16)


def block_scale(own_key, shape, cuts, least, largest):
    level = 1.0
    for axis_at, blocks in cuts:
        draws = jax.random.uniform(jax.random.fold_in(jax.random.fold_in(own_key, 6), axis_at), (blocks,), jnp.float32, least / len(cuts), largest / len(cuts))
        level = level * jnp.repeat(jnp.exp(draws), shape[axis_at] // blocks).reshape((-1,) + (1,) * (len(shape) - 1 - axis_at))
    return level


def gaussian(rng, extent, deviation, reach, shards=(), kind=jnp.bfloat16):
    array = deviation * jax.random.normal(rng, extent, jnp.float32)
    if shards:
        array = array * block_scale(rng, extent, shards, -0.22, 0.18)
    return jnp.clip(array, -reach, reach).astype(kind)


def setup_inputs(seed: int = 0, part: int = 0) -> dict:
    arg_keys = jax.random.split(jax.random.key(seed), 3)
    part_keys = jax.random.split(jax.random.fold_in(arg_keys[2], part), 3)
    panels = draw_panels(jax.random.fold_in(jax.random.fold_in(arg_keys[2], part), 71), part)
    test_matrix = gaussian(arg_keys[1], (N, K), N ** -0.5, 0.0625, ((0, 64),))
    return dict(panels=panels, test_matrix=test_matrix)


def reference(panels, test_matrix):
    count = panels.shape[0]
    stacked = panels.reshape(count * 2 * ROWS, N)
    sketch = jnp.dot(stacked.astype(jnp.float32), test_matrix.astype(jnp.float32), preferred_element_type=jnp.float32)
    sketch = sketch.astype(jnp.bfloat16).reshape(count, 2 * ROWS, K)
    widened = sketch.astype(jnp.float32)
    gram = jnp.einsum('sik,sil->skl', widened, widened, precision=lax.Precision.HIGHEST)
    factor = jnp.linalg.cholesky(gram)
    results = []
    for member in range(count):
        matrix = panels[member].reshape(2 * ROWS, N)
        partial_sum = jnp.dot(matrix.T.astype(jnp.float32), sketch[member].astype(jnp.float32), preferred_element_type=jnp.float32)
        solved = lax.linalg.triangular_solve(factor[member], partial_sum, left_side=False, lower=True, transpose_a=True)
        results.append(solved)
    return jnp.stack(results, axis=1)
```

```python
import functools

import jax
import jax.numpy as jnp
from jax import lax
from jax.experimental import pallas as pl
from jax.experimental.pallas import tpu as pltpu
from jax.sharding import PartitionSpec as P

F32 = jnp.float32
BF16 = jnp.bfloat16
NX, NY, NZ = 4, 2, 8
X_PIECES = ((0, 0, 256), (1, 0, 32))
Z_PIECES = ((1, 32, 256),)
KX = sum(k1 - k0 for _, k0, k1 in X_PIECES)
KZ = sum(k1 - k0 for _, k0, k1 in Z_PIECES)


def scratch():
    dma = pltpu.SemaphoreType.DMA
    buffers = dict(
        om=pltpu.VMEM((NX, NY, NZ, 4, 32, 256), BF16),
        a=pltpu.VMEM((512, 8192), BF16),
        acc=pltpu.VMEM((512, 256), F32),
        st=pltpu.VMEM((2, 256, 256), BF16),
        xs=pltpu.VMEM((2, 2, 8, 2, KX, 128), BF16),
        xr=pltpu.VMEM((2, 2, 8, 2, KX, 128), BF16),
        xacc=pltpu.VMEM((8, 2, KX, 128), F32),
        xy=pltpu.VMEM((8, KX, 128), F32),
        xzs=pltpu.VMEM((2, 4, KX, 128), F32),
        xzr=pltpu.VMEM((2, 4, KX, 128), F32),
        zs=pltpu.VMEM((2, 4, 4, 2, KZ, 128), BF16),
        zr=pltpu.VMEM((2, 4, 4, 2, KZ, 128), BF16),
        zacc=pltpu.VMEM((4, 2, KZ, 128), F32),
        zy=pltpu.VMEM((4, KZ, 128), F32),
        zxs=pltpu.VMEM((2, 2, KZ, 128), F32),
        zxr=pltpu.VMEM((2, 2, KZ, 128), F32),
        gl=pltpu.VMEM((2, 4, 8, 8, 256), F32),
        gy=pltpu.VMEM((4, 8, 8, 256), F32),
        gx=pltpu.VMEM((3, 8, 8, 256), F32),
        gs=pltpu.VMEM((8, 8, 256), F32),
        gz=pltpu.VMEM((7, 8, 256), F32),
        gf=pltpu.VMEM((2, 4, 8, 8, 256), F32),
        a_sem=dma,
        oy=dma((2,)),
        ox=dma((2, 3)),
        oz=dma((2, 2, 4)),
        pz=dma((2, 2, 4)),
        px=dma((2, 3)),
        bz=dma((2, 8)),
        bx=dma((2, 4)),
        x_sem=dma((2, 2, 2, 8)),
        xz_sem=dma((2, 2, 4)),
        xy_sem=dma((2, 8)),
        z_sem=dma((2, 2, 4, 4)),
        zx_sem=dma((2, 2, 2)),
        zy_sem=dma((2, 4)),
        gy_sem=dma((2,)),
        gx_sem=dma((2, 3)),
        gz_sem=dma((2, 7)),
        hz_sem=dma((2, 7)),
        hx_sem=dma((2, 3)),
        hy_sem=dma((2,)),
    )
    return list(buffers), list(buffers.values())


NAMES, SHAPES = scratch()


class Refs:
    pass


def kernel(a_hbm, w_ref, p_out, g_out, *scratch_refs):
    r = Refs()
    for name, ref in zip(NAMES, scratch_refs):
        setattr(r, name, ref)
    me = lax.axis_index("blk")
    fr = lax.axis_index("freq")
    x, y, z, c = me // 16, (me // 8) % 2, me % 8, fr % 2
    d = 1 - 2 * c
    sibling = {"freq": fr + d, "blk": me}

    def at(x_, y_, z_):
        return (((x_ + 8) % 4) * 2 + y_) * 8 + (z_ + 16) % 8

    def to(x_, y_, z_):
        return {"freq": fr, "blk": at(x_, y_, z_)}

    sends = []

    def rc(src, dst, sems, index, device):
        return pltpu.make_async_remote_copy(
            src_ref=src,
            dst_ref=dst,
            send_sem=sems.at[(0,) + index],
            recv_sem=sems.at[(1,) + index],
            device_id=device,
            device_id_type=pl.DeviceIdType.MESH,
        )

    def go(*args):
        copy = rc(*args)
        copy.start()
        sends.append(copy)
        return copy

    copy_a = pltpu.make_async_copy(a_hbm, r.a, r.a_sem)
    copy_a.start()
    r.om[x, y, z, pl.ds(2 * c, 2)] = w_ref[pl.ds(2 * c, 2)]

    barrier = pltpu.get_barrier_semaphore()
    partners = [to(x + o, y, z) for o in range(1, NX)] + [to(x, y, z + o) for o in range(1, NZ)]
    partners += [to(x, 1 - y, z), sibling]
    for partner in partners:
        pl.semaphore_signal(barrier, inc=1, device_id=partner, device_id_type=pl.DeviceIdType.MESH)
    pl.semaphore_wait(barrier, len(partners))

    q0, q1 = 2 * c, 2 * c + 1
    part = r.om.at[x, y, z, pl.ds(2 * c, 2)]
    first = go(part, part, r.oy, (), to(x, 1 - y, z))
    first.wait_recv()

    def slab_pz(zz):
        return r.om.at[x, :, (zz + 16) % 8, q1]

    def slab_oz(zz):
        return r.om.at[:, :, (zz + 16) % 8, q0]

    def slab_px(xx):
        return r.om.at[(xx + 8) % 4, :, :, q1]

    own = r.om.at[x, :, z, q0]
    x_copies = [go(own, own, r.ox, (o - 1,), to(x + o, y, z)) for o in range(1, NX)]

    def hop(slab, sems, way, h, k):
        step = d if way == 0 else -d
        piece = slab(k - step * (h - 1))
        return piece, step

    def z_hop(slab, sems, way, h):
        piece, step = hop(slab, sems, way, h, z)
        return go(piece, piece, sems, (way, h - 1), to(x, y, z + step))

    p_hops = {(way, 1): z_hop(slab_pz, r.pz, way, 1) for way in (0, 1)}
    for copy in x_copies:
        copy.wait_recv()
    o_hops = {(way, 1): z_hop(slab_oz, r.oz, way, 1) for way in (0, 1)}
    b_copies = [go(slab_oz(z), slab_oz(z), r.bz, (0,), sibling)]
    for h in range(1, 5):
        for way in (0, 1):
            if (way, h) in p_hops:
                p_hops[way, h].wait_recv()
                if h < (4 if way == 0 else 3):
                    p_hops[way, h + 1] = z_hop(slab_pz, r.pz, way, h + 1)
        if h == 4:
            piece = slab_px(x)
            px_copies = [
                go(piece, piece, r.px, (0,), to(x + d, y, z)),
                go(piece, piece, r.px, (1,), to(x - d, y, z)),
            ]
            b_copies.append(go(piece, piece, r.bx, (0,), sibling))
        for way in (0, 1):
            if (way, h) in o_hops:
                o_hops[way, h].wait_recv()
                if h < (4 if way == 0 else 3):
                    o_hops[way, h + 1] = z_hop(slab_oz, r.oz, way, h + 1)
                step = d if way == 0 else -d
                piece = slab_oz(z - step * h)
                b_copies.append(go(piece, piece, r.bz, (h if way == 0 else 4 + h,), sibling))
    px_copies[0].wait_recv()
    piece = slab_px(x - d)
    px_copies.append(go(piece, piece, r.px, (2,), to(x + d, y, z)))
    b_copies.append(go(piece, piece, r.bx, (1,), sibling))
    px_copies[1].wait_recv()
    piece = slab_px(x + d)
    b_copies.append(go(piece, piece, r.bx, (2,), sibling))
    px_copies[2].wait_recv()
    piece = slab_px(x - 2 * d)
    b_copies.append(go(piece, piece, r.bx, (3,), sibling))
    copy_a.wait()
    for copy in b_copies:
        copy.wait_recv()

    r.acc[...] = jnp.zeros_like(r.acc)

    @pl.loop(0, 8)
    def _(g):
        columns = pl.ds(pl.multiple_of(g * 1024, 1024), 1024)
        omega = r.om[g // 2, g % 2].reshape(1024, 256)
        r.acc[...] += jnp.dot(r.a[:, columns], omega, preferred_element_type=F32)

    for s in range(2):
        r.st[s] = r.acc[256 * s : 256 * s + 256].astype(BF16).astype(F32).T.astype(BF16)

    def term(pieces, block, received, out):
        columns = pl.ds(pl.multiple_of(block * 128, 128), 128)
        row = 0
        for s, k0, k1 in pieces:
            n = k1 - k0
            value = jnp.dot(r.st[s, k0:k1, :], r.a[256 * s : 256 * s + 256, columns], preferred_element_type=F32)
            for ref in received:
                value = value + ref[row : row + n, :].astype(F32)
            out[row : row + n, :] = value.astype(out.dtype)
            row += n

    def sg(way):
        return 1 - 2 * way

    def z_off(q):
        return 4 + (q // 2) * (1 - q % 2) - ((q + 1) // 2) * (q % 2)

    def x_off(q):
        return 2 - q + 3 * (q // 2) + 2 * (q // 3)

    def x_copy(way, s, q):
        if s == 0:
            src, dst = r.xs.at[way, 0, q, way], r.xr.at[way, 0, q, way]
        else:
            src, dst = r.xs.at[way, 1, q], r.xr.at[way, 1, q]
        return rc(src, dst, r.x_sem, (way, s, q), to(x + sg(way), y, z))

    def x1(q):
        for way in (0, 1):
            term(X_PIECES, at(x + 2, way, z + z_off(q)), [], r.xs.at[way, 0, q, way])
            x_copy(way, 0, q).start()

    def x2(q):
        for way in (0, 1):
            x_copy(way, 0, q).wait_recv()
            for yy in (0, 1):
                got = [r.xr.at[way, 0, q, way]] if yy == way else []
                term(X_PIECES, at(x + sg(way), yy, z + z_off(q)), got, r.xs.at[way, 1, q, yy])
            x_copy(way, 1, q).start()

    def x_fin(q):
        for way in (0, 1):
            x_copy(way, 1, q).wait_recv()
        for yy in (0, 1):
            got = [r.xr.at[way, 1, q, yy] for way in (0, 1)]
            term(X_PIECES, at(x, yy, z + z_off(q)), got, r.xacc.at[q, yy])
        xy_copy(q).start()

    def halves(way, rows):
        return pl.ds(way * (rows // 2), rows // 2)

    def ring_copy(sent, received, sems, way, s, rows, device):
        if s == 0:
            half = halves(way, rows)
            return rc(sent.at[way, 0, half], received.at[way, 0, half], sems, (way, 0), device)
        return rc(sent.at[way, s], received.at[way, s], sems, (way, s), device)

    def ring_step(total, copy, sent, received, s, rows):
        for way in (0, 1):
            if s == 0:
                half = halves(way, rows)
                if way == 0:
                    farthest = total(0)
                sent[way, 0, half] = farthest[way * (rows // 2) : (way + 1) * (rows // 2)]
            else:
                copy(way, s - 1).wait_recv()
                sent[way, s] = total(2 * s - 1 + way)
                half = halves(way, rows) if s == 1 else pl.ds(0, rows)
                sent[way, s, half] += received[way, s - 1, half]
            copy(way, s).start()

    def xy_copy(q):
        return rc(r.xacc.at[q, 1 - y], r.xy.at[q], r.xy_sem, (q,), to(x, 1 - y, z))

    def x_total(q):
        xy_copy(q).wait_recv()
        return r.xacc[q, y] + r.xy[q]

    def xz_copy(way, s):
        return ring_copy(r.xzs, r.xzr, r.xz_sem, way, s, KX, to(x, y, z + sg(way)))

    def xz(s):
        ring_step(x_total, xz_copy, r.xzs, r.xzr, s, KX)

    def z_copy(way, s, q):
        if isinstance(s, int) and s == 0:
            src, dst = r.zs.at[way, 0, q, way], r.zr.at[way, 0, q, way]
        else:
            src, dst = r.zs.at[way, s, q], r.zr.at[way, s, q]
        return rc(src, dst, r.z_sem, (way, s, q), to(x, y, z + sg(way)))

    def z_step(s, q):
        for way in (0, 1):
            far = z + sg(way) * (4 - s)
            if s == 0:
                term(Z_PIECES, at(x + x_off(q), way, far), [], r.zs.at[way, 0, q, way])
            else:
                z_copy(way, s - 1, q).wait_recv()
                for yy in (0, 1):
                    got = [r.zr.at[way, s - 1, q, yy]] if s > 1 or yy == way else []
                    term(Z_PIECES, at(x + x_off(q), yy, far), got, r.zs.at[way, s, q, yy])
            z_copy(way, s, q).start()

    def z_fin(q):
        for way in (0, 1):
            z_copy(way, 3, q).wait_recv()
        for yy in (0, 1):
            got = [r.zr.at[way, 3, q, yy] for way in (0, 1)]
            term(Z_PIECES, at(x + x_off(q), yy, z), got, r.zacc.at[q, yy])
        zy_copy(q).start()

    def zy_copy(q):
        return rc(r.zacc.at[q, 1 - y], r.zy.at[q], r.zy_sem, (q,), to(x, 1 - y, z))

    def z_total(q):
        zy_copy(q).wait_recv()
        return r.zacc[q, y] + r.zy[q]

    def zx_copy(way, s):
        return ring_copy(r.zxs, r.zxr, r.zx_sem, way, s, KZ, to(x + sg(way), y, z))

    def zx(s):
        ring_step(z_total, zx_copy, r.zxs, r.zxr, s, KZ)

    def g_local():
        for s in range(2):
            gram = jnp.dot(r.st[s], r.acc[256 * s : 256 * s + 256].astype(BF16), preferred_element_type=F32)
            r.gl[s] = gram.reshape(4, 8, 8, 256)
        return go(r.gl.at[1 - y], r.gy, r.gy_sem, (), to(x, 1 - y, z))

    def g_x(copy):
        copy.wait_recv()
        r.gy[...] += r.gl[y]
        return [go(r.gy.at[(x + o) % 4], r.gx.at[o - 1], r.gx_sem, (o - 1,), to(x + o, y, z)) for o in range(1, NX)]

    def g_z(copies):
        for copy in copies:
            copy.wait_recv()
        r.gs[...] = r.gy[x] + r.gx[0] + r.gx[1] + r.gx[2]
        return [
            go(r.gs.at[(z + o) % 8], r.gz.at[o - 1], r.gz_sem, (o - 1,), to(x, y, z + o)) for o in range(1, NZ)
        ]

    def h_z(copies):
        for copy in copies:
            copy.wait_recv()
        total = r.gs[z]
        for o in range(1, NZ):
            total = total + r.gz[o - 1]
        r.gf[y, x, z] = total
        piece = r.gf.at[y, x, z]
        return [go(piece, piece, r.hz_sem, (o - 1,), to(x, y, z + o)) for o in range(1, NZ)]

    def h_x(copies):
        for copy in copies:
            copy.wait_recv()
        piece = r.gf.at[y, x]
        return [go(piece, piece, r.hx_sem, (o - 1,), to(x + o, y, z)) for o in range(1, NX)]

    def h_y(copies):
        for copy in copies:
            copy.wait_recv()
        return go(r.gf.at[y], r.gf.at[y], r.hy_sem, (), to(x, 1 - y, z))

    @pl.loop(0, 4)
    def _(j):
        z_step(0, j)
        x1(2 * j)
        x1(2 * j + 1)

    gram = g_local()

    @pl.loop(0, 4)
    def _(j):
        z_step(1, j)
        x2(j)

    gram = g_x(gram)

    @pl.loop(0, 4)
    def _(j):
        x2(4 + j)
        z_step(2, j)

    gram = g_z(gram)
    x_fin(0)
    xz(0)
    gram = h_z(gram)
    z_step(3, 0)
    x_fin(1)
    gram = h_x(gram)
    z_step(3, 1)
    x_fin(2)
    xz(1)
    z_step(3, 2)
    x_fin(3)
    gram = h_y(gram)
    z_step(3, 3)
    z_fin(0)
    zx(0)
    x_fin(4)
    xz(2)
    z_fin(1)
    z_fin(2)
    zx(1)
    x_fin(5)
    z_fin(3)
    x_fin(6)
    xz(3)
    x_fin(7)
    gram.wait_recv()
    g_out[...] = r.gf[...].reshape(2, 256, 256)
    for pieces, total, last, copy, steps, received in (
        (Z_PIECES, z_total, 3, zx_copy, 2, r.zxr),
        (X_PIECES, x_total, 7, xz_copy, 4, r.xzr),
    ):
        value = total(last)
        for way in (0, 1):
            copy(way, steps - 1).wait_recv()
            value = value + received[way, steps - 1]
        row = 0
        for s, k0, k1 in pieces:
            n = k1 - k0
            p_out[s, k0:k1, :] = value[row : row + n]
            row += n

    for copy in sends:
        copy.wait_send()

    @pl.loop(0, 8)
    def _(q):
        xy_copy(q).wait_send()
        for way in (0, 1):
            for s in range(2):
                x_copy(way, s, q).wait_send()

    @pl.loop(0, 4)
    def _(q):
        zy_copy(q).wait_send()
        for way in (0, 1):
            for s in range(4):
                z_copy(way, s, q).wait_send()

    for way in (0, 1):
        for s in range(4):
            xz_copy(way, s).wait_send()
        for s in range(2):
            zx_copy(way, s).wait_send()


def local(panels, test_matrix):
    partial_t, gram = pl.pallas_call(
        kernel,
        out_shape=(jax.ShapeDtypeStruct((2, 256, 128), F32), jax.ShapeDtypeStruct((2, 256, 256), F32)),
        in_specs=[pl.BlockSpec(memory_space=pl.ANY), pl.BlockSpec(memory_space=pltpu.VMEM)],
        out_specs=[pl.BlockSpec(memory_space=pltpu.VMEM)] * 2,
        scratch_shapes=SHAPES,
        compiler_params=pltpu.CompilerParams(
            collective_id=0, has_side_effects=True, vmem_limit_bytes=60 * 1024 * 1024
        ),
    )(panels.reshape(512, 8192), test_matrix.reshape(4, 32, 256))
    factor = jnp.linalg.cholesky(gram)
    results = []
    for member in range(2):
        solved = lax.linalg.triangular_solve(
            factor[member], partial_t[member].T, left_side=False, lower=True, transpose_a=True
        )
        results.append(solved)
    return jnp.stack(results, axis=1)


def solution(mesh):
    in_specs = (P("freq", None, "blk", None), P("blk", None))
    out_specs = P("blk", "freq", None)
    return jax.shard_map(local, mesh=mesh, in_specs=in_specs, out_specs=out_specs, check_vma=False)
```

```python
import functools

import jax
import jax.numpy as jnp
from jax import lax
from jax.experimental import pallas as pl
from jax.experimental.pallas import tpu as pltpu
from jax.sharding import PartitionSpec as P

F32 = jnp.float32
BF16 = jnp.bfloat16
NX, NY, NZ = 4, 2, 8
X_PIECES = ((0, 0, 256), (1, 0, 32))
Z_PIECES = ((1, 32, 256),)
KX = sum(k1 - k0 for _, k0, k1 in X_PIECES)
KZ = sum(k1 - k0 for _, k0, k1 in Z_PIECES)


def scratch():
    dma = pltpu.SemaphoreType.DMA
    buffers = dict(
        om=pltpu.VMEM((NX, NY, NZ, 4, 32, 256), BF16),
        a=pltpu.VMEM((512, 8192), BF16),
        acc=pltpu.VMEM((512, 256), F32),
        st=pltpu.VMEM((2, 256, 256), BF16),
        xs=pltpu.VMEM((2, 2, 8, 2, KX, 128), BF16),
        xr=pltpu.VMEM((2, 2, 8, 2, KX, 128), BF16),
        xacc=pltpu.VMEM((8, 2, KX, 128), F32),
        xy=pltpu.VMEM((8, KX, 128), F32),
        xzs=pltpu.VMEM((2, 4, KX, 128), F32),
        xzr=pltpu.VMEM((2, 4, KX, 128), F32),
        zs=pltpu.VMEM((2, 4, 4, 2, KZ, 128), BF16),
        zr=pltpu.VMEM((2, 4, 4, 2, KZ, 128), BF16),
        zacc=pltpu.VMEM((4, 2, KZ, 128), F32),
        zy=pltpu.VMEM((4, KZ, 128), F32),
        zxs=pltpu.VMEM((2, 2, KZ, 128), F32),
        zxr=pltpu.VMEM((2, 2, KZ, 128), F32),
        gl=pltpu.VMEM((2, 4, 8, 8, 256), F32),
        gy=pltpu.VMEM((4, 8, 8, 256), F32),
        gx=pltpu.VMEM((3, 8, 8, 256), F32),
        gs=pltpu.VMEM((8, 8, 256), F32),
        gz=pltpu.VMEM((7, 8, 256), F32),
        gf=pltpu.VMEM((4, 8, 8, 256), F32),
        m=pltpu.VMEM((256, 512), F32),
        li=pltpu.VMEM((256, 256), F32),
        pt=pltpu.VMEM((2, 256, 128), F32),
        a_sem=dma,
        oxy=dma((2, NX, NY)),
        oz=dma((2, 2, 4, NX)),
        pyz=dma((2, NY, NZ)),
        px=dma((2, 3, NZ)),
        bz=dma((2, 8)),
        bx=dma((2, 4)),
        x_sem=dma((2, 2, 2, 8)),
        xz_sem=dma((2, 2, 4)),
        xy_sem=dma((2, 8)),
        z_sem=dma((2, 2, 4, 4)),
        zx_sem=dma((2, 2, 2)),
        zy_sem=dma((2, 4)),
        gy_sem=dma((2, 4)),
        gx_sem=dma((2, 3)),
        gz_sem=dma((2, 7)),
        hz_sem=dma((2, 7)),
        hx_sem=dma((2, 3)),
        l_sem=dma((2, 8)),
    )
    return list(buffers), list(buffers.values())


NAMES, SHAPES = scratch()


HI = lax.Precision.HIGHEST
PANEL = 32


def factor_group(m, b):
    base = 8 * b
    lanes = 512
    rows = m[base:base+8, :]
    tile = (base // 128) * 128
    sq = m[base:base+8, tile:tile+128]
    l0 = base - tile
    sub = lax.broadcasted_iota(jnp.int32, (8, 128), 0)
    cols = [jnp.broadcast_to(sq[:, l0+k:l0+k+1], (8,128)) for k in range(8)]
    e = [[None]*8 for _ in range(8)]
    for k in range(8):
        for i in range(k, 8):
            e[i][k] = jnp.broadcast_to(cols[k][i:i+1, :], (8,128))
    inv = [None]*8
    r = [[jnp.broadcast_to(rows[i:i+1, 128*t:128*t+128], (8,128)) for t in range(4)] for i in range(8)]
    for k in range(8):
        inv[k] = lax.rsqrt(e[k][k])
        for i in range(k+1, 8):
            e[i][k] = e[i][k] * inv[k]
        for i in range(k+1, 8):
            for j in range(k+1, i+1):
                e[i][j] = e[i][j] - e[i][k]*e[j][k]
    out = [None]*4
    for t in range(4):
        for k in range(8):
            v = r[k][t]
            for j in range(k):
                v = v - e[k][j]*r[j][t]
            r[k][t] = v * inv[k]
        o = r[0][t]
        for k in range(1, 8):
            o = jnp.where(sub == k, r[k][t], o)
        out[t] = o
    u = jnp.concatenate(out, axis=1)
    m[base:base+8, :] = u
    end = (base // PANEL + 1) * PANEL
    if base + 8 < end:
        n = end - base - 8
        coef = u[:, tile:tile+128]
        upd = lax.dot_general(coef, u, (((0,),(0,)),((),())), precision=HI, preferred_element_type=F32)
        m[base+8:end, :] -= upd[base+8-tile:end-tile, :]

def trailing(m, p):
    end = (p+1)*PANEL
    if end >= 256: return
    u = m[end-PANEL:end, :]
    start = (end // 128) * 128
    upd = lax.dot_general(u[:, start:256], u, (((0,),(0,)),((),())), precision=HI, preferred_element_type=F32)
    m[end:256, :] -= upd[end-start:, :]

class Refs:
    pass


SCHEDULE = (
    ("z", 1, 0), ("x2", 0), ("gx", 1), ("z", 1, 1), ("x2", 1), ("gx", 2), ("z", 1, 2), ("x2", 2), ("gx", 3),
    ("z", 1, 3), ("x2", 3), ("gx", 0), ("x2", 4), ("z", 2, 0), ("x2", 5), ("z", 2, 1), ("gz",), ("x2", 6),
    ("z", 2, 2), ("x2", 7), ("z", 2, 3), ("hz",), ("xf", 0), ("z", 3, 0), ("xf", 1), ("z", 3, 1), ("hx",),
    ("z", 3, 2), ("xf", 2), ("xz", 0), ("z", 3, 3), ("xf", 3), ("cs",), ("c", 4), ("xz", 1), ("zf", 0), ("c", 4),
    ("xf", 4), ("zf", 1), ("c", 4), ("xf", 5), ("zf", 2), ("c", 4), ("xz", 2), ("zx", 0), ("xf", 6), ("zf", 3),
    ("c", 5), ("xf", 7), ("zx", 1), ("c", 4), ("xz", 3), ("c", 7),
)


def kernel(a_hbm, w_ref, out, *scratch_refs):
    r = Refs()
    for name, ref in zip(NAMES, scratch_refs):
        setattr(r, name, ref)
    me = lax.axis_index("blk")
    fr = lax.axis_index("freq")
    x, y, z, c = me // 16, (me // 8) % 2, me % 8, fr % 2
    d = 1 - 2 * c
    sibling = {"freq": fr + d, "blk": me}

    def at(x_, y_, z_):
        return (((x_ + 8) % 4) * 2 + y_) * 8 + (z_ + 16) % 8

    def to(x_, y_, z_):
        return {"freq": fr, "blk": at(x_, y_, z_)}

    sends = []

    def rc(src, dst, sems, index, device):
        return pltpu.make_async_remote_copy(
            src_ref=src,
            dst_ref=dst,
            send_sem=sems.at[(0,) + index],
            recv_sem=sems.at[(1,) + index],
            device_id=device,
            device_id_type=pl.DeviceIdType.MESH,
        )

    def go(*args):
        copy = rc(*args)
        copy.start()
        sends.append(copy)
        return copy

    copy_a = pltpu.make_async_copy(a_hbm, r.a, r.a_sem)
    copy_a.start()
    r.om[x, y, z, pl.ds(2 * c, 2)] = w_ref[pl.ds(2 * c, 2)]

    barrier = pltpu.get_barrier_semaphore()
    partners = [to(x + ox, (y + oy) % 2, z) for ox in range(NX) for oy in range(NY) if ox or oy]
    partners += [to(x, (y + oy) % 2, z + oz) for oz in range(1, NZ) for oy in range(NY)]
    partners.append(sibling)
    for partner in partners:
        pl.semaphore_signal(barrier, inc=1, device_id=partner, device_id_type=pl.DeviceIdType.MESH)
    pl.semaphore_wait(barrier, len(partners))

    q0, q1 = 2 * c, 2 * c + 1
    own0, own1 = r.om.at[x, y, z, q0], r.om.at[x, y, z, q1]
    xy_copies, yz_copies = {}, {}

    def xy_first(ox, oy):
        xy_copies[ox, oy] = go(own0, own0, r.oxy, (ox, oy), to(x + ox, (y + oy) % 2, z))

    def yz_first(oz, oy):
        yz_copies[oz, oy] = go(own1, own1, r.pyz, (oy, oz), to(x, (y + oy) % 2, z + oz))

    for step in (
        (xy_first, 0, 1), (yz_first, 0, 1), (xy_first, 1, 0), (xy_first, 3, 0), (yz_first, 1, 0), (yz_first, 7, 0),
        (xy_first, 1, 1), (xy_first, 3, 1), (yz_first, 1, 1), (yz_first, 7, 1), (xy_first, 2, 0), (xy_first, 2, 1),
        (yz_first, 2, 0), (yz_first, 6, 0), (yz_first, 2, 1), (yz_first, 6, 1), (yz_first, 3, 0), (yz_first, 5, 0),
        (yz_first, 3, 1), (yz_first, 5, 1), (yz_first, 4, 0), (yz_first, 4, 1),
    ):
        step[0](*step[1:])

    b_copies, z_hops, x_hops = [], {}, {}

    def z_hop(way, h, ox):
        step = d if way == 0 else -d
        piece = r.om.at[(x + ox) % 4, :, (z - step * (h - 1) + 16) % 8, q0]
        z_hops[way, h, ox] = go(piece, piece, r.oz, (way, h - 1, ox), to(x, y, z + step))

    def x_hop(k, oz):
        xx = x - d if k == 2 else x
        piece = r.om.at[(xx + 8) % 4, :, (z + oz) % 8, q1]
        x_hops[k, oz] = go(piece, piece, r.px, (k, oz), to(x - d if k == 1 else x + d, y, z))

    def z_start(ox):
        for oy in range(NY):
            if ox or oy:
                xy_copies[-ox % NX, oy].wait_recv()
        z_hop(0, 1, ox)
        z_hop(1, 1, ox)

    def x_start(oz):
        for oy in range(NY):
            if oz or oy:
                yz_copies[-oz % NZ, oy].wait_recv()
        x_hop(0, oz)
        x_hop(1, oz)

    def z_next(way, h, ox):
        z_hops[way, h, ox].wait_recv()
        if h < (4 if way == 0 else 3):
            z_hop(way, h + 1, ox)

    def share_z(index, zz):
        piece = r.om.at[:, :, (zz + 16) % 8, q0]
        b_copies.append(go(piece, piece, r.bz, (index,), sibling))

    def share_x(index, xx):
        piece = r.om.at[(xx + 8) % 4, :, :, q1]
        b_copies.append(go(piece, piece, r.bx, (index,), sibling))

    x_order, z_order = (0, 1, 3, 2), (0, 1, 7, 2, 6, 3, 5, 4)
    z_start(0)
    x_start(0)
    z_start(1)
    x_start(1)
    x_start(7)
    z_start(3)
    x_start(2)
    x_start(6)
    z_start(2)
    share_z(0, z)
    for ox in x_order:
        for way in (0, 1):
            z_next(way, 1, ox)
    x_start(3)
    x_start(5)
    x_start(4)
    share_x(0, x)
    share_z(1, z - d)
    share_z(5, z + d)

    def x_next(oz):
        x_hops[0, oz].wait_recv()
        x_hop(2, oz)

    for oz in z_order[:4]:
        x_next(oz)
    for ox in x_order:
        for way in (0, 1):
            z_next(way, 2, ox)
    share_z(2, z - 2 * d)
    share_z(6, z + 2 * d)
    for oz in z_order[4:]:
        x_next(oz)
    share_x(1, x - d)
    for oz in z_order:
        x_hops[1, oz].wait_recv()
    share_x(2, x + d)
    for ox in x_order:
        for way in (0, 1):
            z_next(way, 3, ox)
    share_z(3, z - 3 * d)
    share_z(7, z + 3 * d)
    for oz in z_order:
        x_hops[2, oz].wait_recv()
    share_x(3, x - 2 * d)
    for ox in x_order:
        z_next(0, 4, ox)
    share_z(4, z - 4 * d)
    copy_a.wait()
    for copy in b_copies:
        copy.wait_recv()

    r.acc[...] = jnp.zeros_like(r.acc)

    @pl.loop(0, 8)
    def _(g):
        columns = pl.ds(pl.multiple_of(g * 1024, 1024), 1024)
        omega = r.om[g // 2, g % 2].reshape(1024, 256)
        r.acc[...] += jnp.dot(r.a[:, columns], omega, preferred_element_type=F32)

    for s in range(2):
        r.st[s] = r.acc[256 * s : 256 * s + 256].astype(BF16).astype(F32).T.astype(BF16)

    def term(pieces, block, received, out):
        columns = pl.ds(pl.multiple_of(block * 128, 128), 128)
        row = 0
        for s, k0, k1 in pieces:
            n = k1 - k0
            value = jnp.dot(r.st[s, k0:k1, :], r.a[256 * s : 256 * s + 256, columns], preferred_element_type=F32)
            for ref in received:
                value = value + ref[row : row + n, :].astype(F32)
            out[row : row + n, :] = value.astype(out.dtype)
            row += n

    def sg(way):
        return 1 - 2 * way

    def z_off(q):
        return 4 + (q // 2) * (1 - q % 2) - ((q + 1) // 2) * (q % 2)

    def x_off(q):
        return 2 - q + 3 * (q // 2) + 2 * (q // 3)

    def x_copy(way, s, q):
        if s == 0:
            src, dst = r.xs.at[way, 0, q, way], r.xr.at[way, 0, q, way]
        else:
            src, dst = r.xs.at[way, 1, q], r.xr.at[way, 1, q]
        return rc(src, dst, r.x_sem, (way, s, q), to(x + sg(way), y, z))

    def x1(q):
        for way in (0, 1):
            term(X_PIECES, at(x + 2, way, z + z_off(q)), [], r.xs.at[way, 0, q, way])
            x_copy(way, 0, q).start()

    def x2(q):
        for way in (0, 1):
            x_copy(way, 0, q).wait_recv()
            for yy in (0, 1):
                got = [r.xr.at[way, 0, q, way]] if yy == way else []
                term(X_PIECES, at(x + sg(way), yy, z + z_off(q)), got, r.xs.at[way, 1, q, yy])
            x_copy(way, 1, q).start()

    def x_fin(q):
        for way in (0, 1):
            x_copy(way, 1, q).wait_recv()
        for yy in (0, 1):
            got = [r.xr.at[way, 1, q, yy] for way in (0, 1)]
            term(X_PIECES, at(x, yy, z + z_off(q)), got, r.xacc.at[q, yy])
        xy_copy(q).start()

    def halves(way, rows):
        return pl.ds(way * (rows // 2), rows // 2)

    def ring_copy(sent, received, sems, way, s, rows, device):
        if s == 0:
            half = halves(way, rows)
            return rc(sent.at[way, 0, half], received.at[way, 0, half], sems, (way, 0), device)
        return rc(sent.at[way, s], received.at[way, s], sems, (way, s), device)

    def ring_step(total, copy, sent, received, s, rows):
        for way in (0, 1):
            if s == 0:
                half = halves(way, rows)
                if way == 0:
                    farthest = total(0)
                sent[way, 0, half] = farthest[way * (rows // 2) : (way + 1) * (rows // 2)]
            else:
                copy(way, s - 1).wait_recv()
                sent[way, s] = total(2 * s - 1 + way)
                half = halves(way, rows) if s == 1 else pl.ds(0, rows)
                sent[way, s, half] += received[way, s - 1, half]
            copy(way, s).start()

    def xy_copy(q):
        return rc(r.xacc.at[q, 1 - y], r.xy.at[q], r.xy_sem, (q,), to(x, 1 - y, z))

    def x_total(q):
        xy_copy(q).wait_recv()
        return r.xacc[q, y] + r.xy[q]

    def xz_copy(way, s):
        return ring_copy(r.xzs, r.xzr, r.xz_sem, way, s, KX, to(x, y, z + sg(way)))

    def xz(s):
        ring_step(x_total, xz_copy, r.xzs, r.xzr, s, KX)

    def z_copy(way, s, q):
        if isinstance(s, int) and s == 0:
            src, dst = r.zs.at[way, 0, q, way], r.zr.at[way, 0, q, way]
        else:
            src, dst = r.zs.at[way, s, q], r.zr.at[way, s, q]
        return rc(src, dst, r.z_sem, (way, s, q), to(x, y, z + sg(way)))

    def z_step(s, q):
        for way in (0, 1):
            far = z + sg(way) * (4 - s)
            if s == 0:
                term(Z_PIECES, at(x + x_off(q), way, far), [], r.zs.at[way, 0, q, way])
            else:
                z_copy(way, s - 1, q).wait_recv()
                for yy in (0, 1):
                    got = [r.zr.at[way, s - 1, q, yy]] if s > 1 or yy == way else []
                    term(Z_PIECES, at(x + x_off(q), yy, far), got, r.zs.at[way, s, q, yy])
            z_copy(way, s, q).start()

    def z_fin(q):
        for way in (0, 1):
            z_copy(way, 3, q).wait_recv()
        for yy in (0, 1):
            got = [r.zr.at[way, 3, q, yy] for way in (0, 1)]
            term(Z_PIECES, at(x + x_off(q), yy, z), got, r.zacc.at[q, yy])
        zy_copy(q).start()

    def zy_copy(q):
        return rc(r.zacc.at[q, 1 - y], r.zy.at[q], r.zy_sem, (q,), to(x, 1 - y, z))

    def z_total(q):
        zy_copy(q).wait_recv()
        return r.zacc[q, y] + r.zy[q]

    def zx_copy(way, s):
        return ring_copy(r.zxs, r.zxr, r.zx_sem, way, s, KZ, to(x + sg(way), y, z))

    def zx(s):
        ring_step(z_total, zx_copy, r.zxs, r.zxr, s, KZ)

    gram = {}

    def g_local():
        for s in range(2):
            value = jnp.dot(r.st[s], r.acc[256 * s : 256 * s + 256].astype(BF16), preferred_element_type=F32)
            r.gl[s] = value.reshape(4, 8, 8, 256)
        for o in (1, 2, 3, 0):
            k = (x + o) % 4
            gram["y", o] = go(r.gl.at[1 - y, k], r.gy.at[k], r.gy_sem, (o,), to(x, 1 - y, z))

    def g_x(o):
        gram["y", o].wait_recv()
        k = (x + o) % 4
        r.gy[k] += r.gl[y, k]
        if o:
            gram["x", o] = go(r.gy.at[k], r.gx.at[o - 1], r.gx_sem, (o - 1,), to(x + o, y, z))

    def g_z():
        for o in range(1, NX):
            gram["x", o].wait_recv()
        r.gs[...] = r.gy[x] + r.gx[0] + r.gx[1] + r.gx[2]
        for o in range(1, NZ):
            gram["z", o] = go(r.gs.at[(z + o) % 8], r.gz.at[o - 1], r.gz_sem, (o - 1,), to(x, y, z + o))

    def h_z():
        for o in range(1, NZ):
            gram["z", o].wait_recv()
        total = r.gs[z]
        for o in range(1, NZ):
            total = total + r.gz[o - 1]
        r.gf[x, z] = total
        piece = r.gf.at[x, z]
        for o in range(1, NZ):
            gram["hz", o] = go(piece, piece, r.hz_sem, (o - 1,), to(x, y, z + o))

    def h_x():
        for o in range(1, NZ):
            gram["hz", o].wait_recv()
        piece = r.gf.at[x]
        for o in range(1, NX):
            gram["hx", o] = go(piece, piece, r.hx_sem, (o - 1,), to(x + o, y, z))

    def c_start():
        for o in range(1, NX):
            gram["hx", o].wait_recv()
        r.m[:, :256] = r.gf[...].reshape(256, 256)
        row = lax.broadcasted_iota(jnp.int32, (256, 256), 0)
        column = lax.broadcasted_iota(jnp.int32, (256, 256), 1)
        r.m[:, 256:] = jnp.where(row == column, 1.0, 0.0).astype(F32)

    l_copies = []

    def c_group(b):
        factor_group(r.m, b)
        if (8 * b + 8) % PANEL == 0:
            p = 8 * b // PANEL
            trailing(r.m, p)
            rows = slice(PANEL * p, PANEL * p + PANEL)
            l_copies.append(go(r.m.at[rows, 256:512], r.li.at[rows], r.l_sem, (p,), to(x, 1 - y, z)))

    g_local()

    @pl.loop(0, 4)
    def _(j):
        z_step(0, j)
        x1(2 * j)
        x1(2 * j + 1)

    groups = iter(range(32))

    def c_next(n):
        for b in [b for _, b in zip(range(n), groups)]:
            c_group(b)

    steps = dict(
        z=z_step, x2=x2, gx=g_x, gz=g_z, hz=h_z, hx=h_x, xf=x_fin, zf=z_fin, xz=xz, zx=zx, cs=c_start, c=c_next
    )
    for name, *args in SCHEDULE:
        steps[name](*args)

    for pieces, total, last, copy, steps, received in (
        (Z_PIECES, z_total, 3, zx_copy, 2, r.zxr),
        (X_PIECES, x_total, 7, xz_copy, 4, r.xzr),
    ):
        value = total(last)
        for way in (0, 1):
            copy(way, steps - 1).wait_recv()
            value = value + received[way, steps - 1]
        row = 0
        for s, k0, k1 in pieces:
            n = k1 - k0
            r.pt[s, k0:k1, :] = value[row : row + n]
            row += n

    def solved(s, inverse):
        out[s] = lax.dot_general(
            r.pt[s], inverse, (((0,), (1,)), ((), ())), precision=HI, preferred_element_type=F32
        )

    solved(y, r.m[:, 256:])
    for copy in l_copies:
        copy.wait_recv()
    solved(1 - y, r.li[...])

    for copy in sends:
        copy.wait_send()

    @pl.loop(0, 8)
    def _(q):
        xy_copy(q).wait_send()
        for way in (0, 1):
            for s in range(2):
                x_copy(way, s, q).wait_send()

    @pl.loop(0, 4)
    def _(q):
        zy_copy(q).wait_send()
        for way in (0, 1):
            for s in range(4):
                z_copy(way, s, q).wait_send()

    for way in (0, 1):
        for s in range(4):
            xz_copy(way, s).wait_send()
        for s in range(2):
            zx_copy(way, s).wait_send()


def local(panels, test_matrix):
    projected = pl.pallas_call(
        kernel,
        out_shape=jax.ShapeDtypeStruct((2, 128, 256), F32),
        in_specs=[pl.BlockSpec(memory_space=pl.ANY), pl.BlockSpec(memory_space=pltpu.VMEM)],
        out_specs=pl.BlockSpec(memory_space=pltpu.VMEM),
        scratch_shapes=SHAPES,
        compiler_params=pltpu.CompilerParams(
            collective_id=0, has_side_effects=True, vmem_limit_bytes=60 * 1024 * 1024
        ),
    )(panels.reshape(512, 8192), test_matrix.reshape(4, 32, 256))
    return projected.transpose(1, 0, 2)


def solution(mesh):
    in_specs = (P("freq", None, "blk", None), P("blk", None))
    out_specs = P("blk", "freq", None)
    return jax.shard_map(local, mesh=mesh, in_specs=in_specs, out_specs=out_specs, check_vma=False)
```

```python
import functools

import jax
import jax.numpy as jnp
from jax import lax
from jax.experimental import pallas as pl
from jax.experimental.pallas import tpu as pltpu
from jax.sharding import PartitionSpec as P

F32 = jnp.float32
BF16 = jnp.bfloat16
NX, NY, NZ = 4, 2, 8
X_PIECES = ((0, 0, 256), (1, 0, 16))
Z_PIECES = ((1, 16, 256),)
OFFSETS = (0, 1, 7, 2, 6, 3, 5, 4)
X_GROUPS = ((0, 1), (1, 3), (3, 5), (5, 7), (7, 8))
Y_GROUPS = ((0, 3), (3, 5), (5, 8))
KX = sum(k1 - k0 for _, k0, k1 in X_PIECES)
KZ = sum(k1 - k0 for _, k0, k1 in Z_PIECES)


def scratch():
    dma = pltpu.SemaphoreType.DMA
    buffers = dict(
        om=pltpu.VMEM((NX, NY, NZ, 4, 32, 256), BF16),
        a=pltpu.VMEM((512, 8192), BF16),
        acc=pltpu.VMEM((512, 256), F32),
        st=pltpu.VMEM((2, 256, 256), BF16),
        xs=pltpu.VMEM((2, 2, 8, 2, KX, 128), BF16),
        xr=pltpu.VMEM((2, 2, 8, 2, KX, 128), BF16),
        xacc=pltpu.VMEM((8, 2, KX, 128), F32),
        xys=pltpu.VMEM((8, KX, 128), BF16),
        xy=pltpu.VMEM((8, KX, 128), BF16),
        xzs=pltpu.VMEM((2, 4, KX, 128), F32),
        xzr=pltpu.VMEM((2, 4, KX, 128), F32),
        zs=pltpu.VMEM((2, 4, 4, 2, KZ, 128), BF16),
        zr=pltpu.VMEM((2, 4, 4, 2, KZ, 128), BF16),
        zacc=pltpu.VMEM((4, 2, KZ, 128), F32),
        zy=pltpu.VMEM((4, KZ, 128), F32),
        zxs=pltpu.VMEM((2, 2, KZ, 128), F32),
        zxr=pltpu.VMEM((2, 2, KZ, 128), F32),
        gl=pltpu.VMEM((2, 4, 8, 8, 256), F32),
        gy=pltpu.VMEM((4, 8, 8, 256), F32),
        gx=pltpu.VMEM((3, 8, 8, 256), F32),
        gs=pltpu.VMEM((8, 8, 256), F32),
        gz=pltpu.VMEM((7, 8, 256), F32),
        gf=pltpu.VMEM((4, 8, 8, 256), F32),
        m=pltpu.VMEM((256, 512), F32),
        li=pltpu.VMEM((256, 256), F32),
        pt=pltpu.VMEM((2, 256, 128), F32),
        a_sem=dma,
        oz=dma((2, NZ)),
        ox=dma((2, 3, 5)),
        oy=dma((2, 2, NX, 3)),
        ob=dma((2, 2, NX)),
        x_sem=dma((2, 2, 2, 8)),
        xz_sem=dma((2, 2, 4)),
        xy_sem=dma((2, 8)),
        z_sem=dma((2, 2, 4, 4)),
        zx_sem=dma((2, 2, 2)),
        zy_sem=dma((2, 4)),
        gy_sem=dma((2, 4)),
        gx_sem=dma((2, 3)),
        gz_sem=dma((2, 7)),
        hz_sem=dma((2, 7)),
        hx_sem=dma((2, 3)),
        l_sem=dma((2, 8)),
    )
    return list(buffers), list(buffers.values())


NAMES, SHAPES = scratch()


HI = lax.Precision.HIGHEST
PANEL = 32


def factor_group(m, b):
    base = 8 * b
    tile = base // 128
    l0 = base - 128 * tile
    tiles = (0, 1, 2) if tile == 0 else (1, 2, 3)
    end = (base // PANEL + 1) * PANEL
    sub = lax.broadcasted_iota(jnp.int32, (8, 128), 0)

    def full(v):
        return jnp.broadcast_to(v, (8, 128))

    square = m[base:base+8, 128*tile:128*tile+128]
    below = [m[g:g+8, 128*tile:128*tile+128] for g in range(base+8, end, 8)]
    cols = [full(square[:, l0+k:l0+k+1]) for k in range(8)]
    e = [[full(cols[k][i:i+1]) if i >= k else None for k in range(8)] for i in range(8)]
    lower = [[full(g[:, l0+k:l0+k+1]) for k in range(8)] for g in below]
    inv = [None]*8
    for k in range(8):
        inv[k] = lax.rsqrt(e[k][k])
        for i in range(k+1, 8):
            e[i][k] = e[i][k] * inv[k]
        for i in range(k+1, 8):
            for j in range(k+1, i+1):
                e[i][j] = e[i][j] - e[i][k]*e[j][k]
    for g in lower:
        for k in range(8):
            v = g[k]
            for j in range(k):
                v = v - g[j]*e[k][j]
            g[k] = v*inv[k]
    for t in tiles:
        lanes = slice(128*t, 128*t+128)
        rows = m[base:base+8, lanes]
        u = []
        for k in range(8):
            v = full(rows[k:k+1])
            for j in range(k):
                v = v - e[k][j]*u[j]
            u.append(v*inv[k])
        o = u[0]
        for k in range(1, 8):
            o = jnp.where(sub == k, u[k], o)
        m[base:base+8, lanes] = o
        for n, g in enumerate(lower):
            r0 = base+8+8*n
            v = m[r0:r0+8, lanes]
            for k in range(8):
                v = v - g[k]*u[k]
            m[r0:r0+8, lanes] = v

def trailing(m, p):
    end = (p+1)*PANEL
    if end >= 256:
        return
    u0 = m[end-PANEL:end, :]
    for half in (0, 1):
        lo, hi = max(end, 128*half), 128*half+128
        if lo >= hi:
            continue
        first = 128*half
        last = 384 if end <= 128 else 512
        upd = lax.dot_general(u0[:, 128*half:hi], u0[:, first:last], (((0,),(0,)),((),())), precision=HI, preferred_element_type=F32)
        m[lo:hi, first:last] -= upd[lo-128*half:]


class Refs:
    pass


SCHEDULE = (
    ("z", 0, 1), ("gl",), ("x1", 1), ("z", 0, 0), ("x1", 0), ("z", 0, 3), ("z", 1, 1), ("gx", 1), ("x2", 1),
    ("z", 1, 0), ("gx", 2), ("z", 1, 3), ("x2", 0), ("gx", 3), ("x1", 3), ("gx", 0), ("z", 2, 1), ("x1", 2),
    ("x1", 4), ("x1", 6), ("z", 0, 2), ("z", 2, 3), ("gz",), ("x1", 5), ("xf", 0), ("z", 3, 1), ("z", 1, 2),
    ("xf", 1), ("x2", 3), ("x2", 2), ("z", 2, 0), ("z", 3, 3), ("xz", 0), ("x2", 4), ("x2", 6), ("x2", 5), ("hz",),
    ("zf", 1), ("xf", 3), ("x1", 7), ("z", 2, 2), ("xf", 2), ("z", 3, 0), ("zf", 3), ("xf", 4), ("xz", 1), ("xf", 6),
    ("hx",), ("z", 3, 2), ("xf", 5), ("x2", 7), ("zf", 0), ("xz", 2), ("cs",), ("c", 3), ("zx", 0), ("c", 1),
    ("zf", 2), ("c", 1), ("xf", 7), ("c", 7), ("xz", 3), ("c", 6), ("zx", 1), ("c", 14),
)


def kernel(a_hbm, w_ref, out, *scratch_refs):
    r = Refs()
    for name, ref in zip(NAMES, scratch_refs):
        setattr(r, name, ref)
    me = lax.axis_index("blk")
    fr = lax.axis_index("freq")
    x, y, z, c = me // 16, (me // 8) % 2, me % 8, fr % 2
    d = 1 - 2 * c
    sibling = {"freq": fr + d, "blk": me}

    def at(x_, y_, z_):
        return (((x_ + 8) % 4) * 2 + y_) * 8 + (z_ + 16) % 8

    def to(x_, y_, z_):
        return {"freq": fr, "blk": at(x_, y_, z_)}

    sends = []

    def rc(src, dst, sems, index, device):
        return pltpu.make_async_remote_copy(
            src_ref=src,
            dst_ref=dst,
            send_sem=sems.at[(0,) + index],
            recv_sem=sems.at[(1,) + index],
            device_id=device,
            device_id_type=pl.DeviceIdType.MESH,
        )

    def go(*args):
        copy = rc(*args)
        copy.start()
        sends.append(copy)
        return copy

    copy_a = pltpu.make_async_copy(a_hbm, r.a, r.a_sem)
    copy_a.start()
    half = pl.ds(2 * c, 2)
    r.om[x, y, 0, half] = w_ref[half]

    barrier = pltpu.get_barrier_semaphore()
    across = {"freq": (fr + 2) % 4, "blk": at(x, 1 - y, z)}
    partners = [to(x + o, y, z) for o in range(1, NX)] + [to(x, y, z + o) for o in range(1, NZ)]
    partners += [to(x, 1 - y, z), across, sibling]
    for partner in partners:
        pl.semaphore_signal(barrier, inc=1, device_id=partner, device_id_type=pl.DeviceIdType.MESH)
    pl.semaphore_wait(barrier, len(partners))

    z_copies, x_copies, y_copies, b_copies = {}, {}, {}, {}

    def z_send(oz):
        k = OFFSETS.index(-oz % NZ)
        z_copies[k] = go(r.om.at[x, y, 0, half], r.om.at[x, y, k, half], r.oz, (k,), to(x, y, z + oz))

    def z_pass():
        z_copies[5].wait_recv()
        z_copies[6].wait_recv()
        z_copies[7] = go(r.om.at[x, y, 6 - c, half], r.om.at[x, y, 7, half], r.oz, (7,), to(x, y, z + d))

    def slab_x(xi):
        return (x + (0, -d, d, 2)[xi] + 4) % 4

    def x_send(g, k):
        a, b = X_GROUPS[g]
        if k == 2:
            x_copies[g, 0].wait_recv()
        piece = r.om.at[slab_x(1 if k == 2 else 0), y, a:b, half]
        x_copies[g, k] = go(piece, piece, r.ox, (k, g), to(x - d if k == 1 else x + d, y, z))

    def y_send(xi, g):
        a, b = Y_GROUPS[g]
        for side, device in enumerate((to(x, 1 - y, z), across)):
            piece = r.om.at[slab_x(xi), y, a:b, 2 * c + side]
            y_copies[xi, g, side] = go(piece, piece, r.oy, (side, xi, g), device)

    def share(xi, yi):
        if yi:
            for g in range(3):
                for side in (0, 1):
                    y_copies[xi, g, side].wait_recv()
        index = (yi, (0, 2, 1, 3)[xi])
        piece = r.om.at[slab_x(xi), y if yi == 0 else 1 - y, :, half]
        b_copies[index] = go(piece, piece, r.ob, index, sibling)

    def own(ranks):
        for k in ranks:
            z_copies[k].wait_recv()

    def got(k, groups):
        for g in groups:
            x_copies[g, k].wait_recv()

    def sketch(xi, yi, first=False):
        b_copies[yi, xi].wait_recv()
        xx, yy = slab_x(xi), y if yi == 0 else 1 - y
        columns = [r.a[:, pl.ds(pl.multiple_of(at(xx, yy, z + o) * 128, 128), 128)] for o in OFFSETS]
        omega = r.om[xx, yy].reshape(1024, 256)
        value = jnp.dot(jnp.concatenate(columns, axis=1), omega, preferred_element_type=F32)
        r.acc[...] = value if first else r.acc[...] + value

    for o in (1, 7, 2, 6, 3, 5):
        z_send(o)
    x_send(0, 0)
    x_send(0, 1)
    own((1, 2))
    x_send(1, 0)
    x_send(1, 1)
    y_send(0, 0)
    own((3, 4))
    x_send(2, 0)
    x_send(2, 1)
    y_send(0, 1)
    x_send(0, 2)
    z_pass()
    x_send(3, 0)
    x_send(3, 1)
    x_send(1, 2)
    y_send(1, 0)
    got(1, (0, 1))
    y_send(2, 0)
    own((7,))
    x_send(4, 0)
    x_send(4, 1)
    y_send(0, 2)
    share(0, 0)
    x_send(2, 2)
    y_send(1, 1)
    got(1, (2,))
    y_send(2, 1)
    x_send(3, 2)
    x_send(4, 2)
    y_send(1, 2)
    share(1, 0)
    got(1, (3, 4))
    y_send(2, 2)
    share(2, 0)
    got(2, (0, 1))
    y_send(3, 0)
    got(2, (2,))
    y_send(3, 1)
    got(2, (3, 4))
    y_send(3, 2)
    share(3, 0)
    copy_a.wait()
    sketch(0, 0, True)
    share(0, 1)
    sketch(1, 0)
    share(1, 1)
    sketch(2, 0)
    share(2, 1)
    sketch(3, 0)
    sketch(0, 1)
    sketch(1, 1)
    share(3, 1)
    sketch(2, 1)
    sketch(3, 1)

    for s in range(2):
        r.st[s] = r.acc[256 * s : 256 * s + 256].astype(BF16).astype(F32).T.astype(BF16)

    def term(pieces, block, received, out):
        columns = pl.ds(pl.multiple_of(block * 128, 128), 128)
        row = 0
        for s, k0, k1 in pieces:
            n = k1 - k0
            value = jnp.dot(r.st[s, k0:k1, :], r.a[256 * s : 256 * s + 256, columns], preferred_element_type=F32)
            for ref in received:
                value = value + ref[row : row + n, :].astype(F32)
            out[row : row + n, :] = value.astype(out.dtype)
            row += n

    def sg(way):
        return 1 - 2 * way

    def z_off(q):
        return 4 + (q // 2) * (1 - q % 2) - ((q + 1) // 2) * (q % 2)

    def x_off(q):
        return 2 - q + 3 * (q // 2) + 2 * (q // 3)

    def x_copy(way, s, q):
        if s == 0:
            src, dst = r.xs.at[way, 0, q, way], r.xr.at[way, 0, q, way]
        else:
            src, dst = r.xs.at[way, 1, q], r.xr.at[way, 1, q]
        return rc(src, dst, r.x_sem, (way, s, q), to(x + sg(way), y, z))

    def x1(q):
        for way in (0, 1):
            term(X_PIECES, at(x + 2, way, z + z_off(q)), [], r.xs.at[way, 0, q, way])
            x_copy(way, 0, q).start()

    def x2(q):
        for way in (0, 1):
            x_copy(way, 0, q).wait_recv()
            for yy in (0, 1):
                got = [r.xr.at[way, 0, q, way]] if yy == way else []
                term(X_PIECES, at(x + sg(way), yy, z + z_off(q)), got, r.xs.at[way, 1, q, yy])
            x_copy(way, 1, q).start()

    def x_fin(q):
        for way in (0, 1):
            x_copy(way, 1, q).wait_recv()
        for yy in (0, 1):
            got = [r.xr.at[way, 1, q, yy] for way in (0, 1)]
            term(X_PIECES, at(x, yy, z + z_off(q)), got, r.xacc.at[q, yy])
        r.xys[q] = r.xacc[q, 1 - y].astype(BF16)
        xy_copy(q).start()

    def halves(way, rows):
        return pl.ds(way * (rows // 2), rows // 2)

    def ring_copy(sent, received, sems, way, s, rows, device):
        if s == 0:
            half = halves(way, rows)
            return rc(sent.at[way, 0, half], received.at[way, 0, half], sems, (way, 0), device)
        return rc(sent.at[way, s], received.at[way, s], sems, (way, s), device)

    def ring_step(total, copy, sent, received, s, rows):
        for way in (0, 1):
            if s == 0:
                half = halves(way, rows)
                if way == 0:
                    farthest = total(0)
                sent[way, 0, half] = farthest[way * (rows // 2) : (way + 1) * (rows // 2)]
            else:
                copy(way, s - 1).wait_recv()
                sent[way, s] = total(2 * s - 1 + way)
                half = halves(way, rows) if s == 1 else pl.ds(0, rows)
                sent[way, s, half] += received[way, s - 1, half]
            copy(way, s).start()

    def xy_copy(q):
        return rc(r.xys.at[q], r.xy.at[q], r.xy_sem, (q,), to(x, 1 - y, z))

    def x_total(q):
        xy_copy(q).wait_recv()
        return r.xacc[q, y] + r.xy[q].astype(F32)

    def xz_copy(way, s):
        return ring_copy(r.xzs, r.xzr, r.xz_sem, way, s, KX, to(x, y, z + sg(way)))

    def xz(s):
        ring_step(x_total, xz_copy, r.xzs, r.xzr, s, KX)

    def z_copy(way, s, q):
        if isinstance(s, int) and s == 0:
            src, dst = r.zs.at[way, 0, q, way], r.zr.at[way, 0, q, way]
        else:
            src, dst = r.zs.at[way, s, q], r.zr.at[way, s, q]
        return rc(src, dst, r.z_sem, (way, s, q), to(x, y, z + sg(way)))

    def z_step(s, q):
        for way in (0, 1):
            far = z + sg(way) * (4 - s)
            if s == 0:
                term(Z_PIECES, at(x + x_off(q), way, far), [], r.zs.at[way, 0, q, way])
            else:
                z_copy(way, s - 1, q).wait_recv()
                for yy in (0, 1):
                    got = [r.zr.at[way, s - 1, q, yy]] if s > 1 or yy == way else []
                    term(Z_PIECES, at(x + x_off(q), yy, far), got, r.zs.at[way, s, q, yy])
            z_copy(way, s, q).start()

    def z_fin(q):
        for way in (0, 1):
            z_copy(way, 3, q).wait_recv()
        for yy in (0, 1):
            got = [r.zr.at[way, 3, q, yy] for way in (0, 1)]
            term(Z_PIECES, at(x + x_off(q), yy, z), got, r.zacc.at[q, yy])
        zy_copy(q).start()

    def zy_copy(q):
        return rc(r.zacc.at[q, 1 - y], r.zy.at[q], r.zy_sem, (q,), to(x, 1 - y, z))

    def z_total(q):
        zy_copy(q).wait_recv()
        return r.zacc[q, y] + r.zy[q]

    def zx_copy(way, s):
        return ring_copy(r.zxs, r.zxr, r.zx_sem, way, s, KZ, to(x + sg(way), y, z))

    def zx(s):
        ring_step(z_total, zx_copy, r.zxs, r.zxr, s, KZ)

    gram = {}

    def g_local():
        for s in range(2):
            value = jnp.dot(r.st[s], r.acc[256 * s : 256 * s + 256].astype(BF16), preferred_element_type=F32)
            r.gl[s] = value.reshape(4, 8, 8, 256)
        for o in (1, 2, 3, 0):
            k = (x + o) % 4
            gram["y", o] = go(r.gl.at[1 - y, k], r.gy.at[k], r.gy_sem, (o,), to(x, 1 - y, z))

    def g_x(o):
        gram["y", o].wait_recv()
        k = (x + o) % 4
        r.gy[k] += r.gl[y, k]
        if o:
            gram["x", o] = go(r.gy.at[k], r.gx.at[o - 1], r.gx_sem, (o - 1,), to(x + o, y, z))

    def g_z():
        for o in range(1, NX):
            gram["x", o].wait_recv()
        r.gs[...] = r.gy[x] + r.gx[0] + r.gx[1] + r.gx[2]
        for o in range(1, NZ):
            gram["z", o] = go(r.gs.at[(z + o) % 8], r.gz.at[o - 1], r.gz_sem, (o - 1,), to(x, y, z + o))

    def h_z():
        for o in range(1, NZ):
            gram["z", o].wait_recv()
        total = r.gs[z]
        for o in range(1, NZ):
            total = total + r.gz[o - 1]
        r.gf[x, z] = total
        piece = r.gf.at[x, z]
        for o in range(1, NZ):
            gram["hz", o] = go(piece, piece, r.hz_sem, (o - 1,), to(x, y, z + o))

    def h_x():
        for o in range(1, NZ):
            gram["hz", o].wait_recv()
        piece = r.gf.at[x]
        for o in range(1, NX):
            gram["hx", o] = go(piece, piece, r.hx_sem, (o - 1,), to(x + o, y, z))

    def c_start():
        for o in range(1, NX):
            gram["hx", o].wait_recv()
        r.m[:, :256] = r.gf[...].reshape(256, 256)
        row = lax.broadcasted_iota(jnp.int32, (256, 256), 0)
        column = lax.broadcasted_iota(jnp.int32, (256, 256), 1)
        r.m[:, 256:] = jnp.where(row == column, 1.0, 0.0).astype(F32)

    l_copies = []

    def c_group(b):
        factor_group(r.m, b)
        if (8 * b + 8) % PANEL == 0:
            p = 8 * b // PANEL
            trailing(r.m, p)
            rows = slice(PANEL * p, PANEL * p + PANEL)
            l_copies.append(go(r.m.at[rows, 256:512], r.li.at[rows], r.l_sem, (p,), to(x, 1 - y, z)))

    groups = iter(range(32))

    def c_next(n):
        for b in [b for _, b in zip(range(n), groups)]:
            c_group(b)

    steps = dict(
        gl=g_local, z=z_step, x1=x1, x2=x2, gx=g_x, gz=g_z, hz=h_z, hx=h_x, xf=x_fin, zf=z_fin, xz=xz, zx=zx, cs=c_start, c=c_next
    )
    for name, *args in SCHEDULE:
        steps[name](*args)

    for pieces, total, last, copy, steps, received in (
        (Z_PIECES, z_total, 3, zx_copy, 2, r.zxr),
        (X_PIECES, x_total, 7, xz_copy, 4, r.xzr),
    ):
        value = total(last)
        for way in (0, 1):
            copy(way, steps - 1).wait_recv()
            value = value + received[way, steps - 1]
        row = 0
        for s, k0, k1 in pieces:
            n = k1 - k0
            r.pt[s, k0:k1, :] = value[row : row + n]
            row += n

    def solved(s, inverse):
        out[s] = lax.dot_general(
            r.pt[s], inverse, (((0,), (1,)), ((), ())), precision=HI, preferred_element_type=F32
        )

    solved(y, r.m[:, 256:])
    for copy in l_copies:
        copy.wait_recv()
    solved(1 - y, r.li[...])

    for copy in sends:
        copy.wait_send()

    @pl.loop(0, 8)
    def _(q):
        xy_copy(q).wait_send()
        for way in (0, 1):
            for s in range(2):
                x_copy(way, s, q).wait_send()

    @pl.loop(0, 4)
    def _(q):
        zy_copy(q).wait_send()
        for way in (0, 1):
            for s in range(4):
                z_copy(way, s, q).wait_send()

    for way in (0, 1):
        for s in range(4):
            xz_copy(way, s).wait_send()
        for s in range(2):
            zx_copy(way, s).wait_send()


def local(panels, test_matrix):
    projected = pl.pallas_call(
        kernel,
        out_shape=jax.ShapeDtypeStruct((2, 128, 256), F32),
        in_specs=[pl.BlockSpec(memory_space=pl.ANY), pl.BlockSpec(memory_space=pltpu.VMEM)],
        out_specs=pl.BlockSpec(memory_space=pltpu.VMEM),
        scratch_shapes=SHAPES,
        compiler_params=pltpu.CompilerParams(
            collective_id=0, has_side_effects=True, vmem_limit_bytes=60 * 1024 * 1024
        ),
    )(panels.reshape(512, 8192), test_matrix.reshape(4, 32, 256))
    return projected.transpose(1, 0, 2)


def solution(mesh):
    in_specs = (P("freq", None, "blk", None), P("blk", None))
    out_specs = P("blk", "freq", None)
    return jax.shard_map(local, mesh=mesh, in_specs=in_specs, out_specs=out_specs, check_vma=False)
```

```python
import functools

import jax
import jax.numpy as jnp
from jax import lax
from jax.experimental import pallas as pl
from jax.experimental.pallas import tpu as pltpu
from jax.sharding import PartitionSpec as P

F32 = jnp.float32
BF16 = jnp.bfloat16
NX, NY, NZ = 4, 2, 8
X_PIECES = ((0, 0, 256), (1, 0, 16))
Z_PIECES = ((1, 16, 256),)
OFFSETS = (0, 1, 7, 2, 6, 3, 5, 4)
X_GROUPS = ((0, 1), (1, 3), (3, 5), (5, 7), (7, 8))
Y_GROUPS = ((0, 3), (3, 5), (5, 8))
KX = sum(k1 - k0 for _, k0, k1 in X_PIECES)
KZ = sum(k1 - k0 for _, k0, k1 in Z_PIECES)


def scratch():
    dma = pltpu.SemaphoreType.DMA
    buffers = dict(
        om=pltpu.VMEM((NX, NY, NZ, 4, 32, 256), BF16),
        a=pltpu.VMEM((512, 8192), BF16),
        acc=pltpu.VMEM((512, 256), F32),
        st=pltpu.VMEM((2, 256, 256), BF16),
        xs=pltpu.VMEM((2, 2, 8, 2, KX, 128), BF16),
        xr=pltpu.VMEM((2, 2, 8, 2, KX, 128), BF16),
        xacc=pltpu.VMEM((8, 2, KX, 128), F32),
        xys=pltpu.VMEM((8, KX, 128), BF16),
        xy=pltpu.VMEM((8, KX, 128), BF16),
        xzs=pltpu.VMEM((2, 4, KX, 128), F32),
        xzr=pltpu.VMEM((2, 4, KX, 128), F32),
        zs=pltpu.VMEM((2, 4, 4, 2, KZ, 128), BF16),
        zr=pltpu.VMEM((2, 4, 4, 2, KZ, 128), BF16),
        zacc=pltpu.VMEM((4, 2, KZ, 128), F32),
        zy=pltpu.VMEM((4, KZ, 128), F32),
        zxs=pltpu.VMEM((2, 2, KZ, 128), F32),
        zxr=pltpu.VMEM((2, 2, KZ, 128), F32),
        gl=pltpu.VMEM((2, 4, 8, 8, 256), F32),
        gy=pltpu.VMEM((4, 8, 8, 256), F32),
        gx=pltpu.VMEM((3, 8, 8, 256), F32),
        gs=pltpu.VMEM((8, 8, 256), F32),
        gz=pltpu.VMEM((7, 8, 256), F32),
        gf=pltpu.VMEM((4, 8, 8, 256), F32),
        m=pltpu.VMEM((256, 512), F32),
        li=pltpu.VMEM((256, 256), F32),
        pt=pltpu.VMEM((2, 256, 128), F32),
        a_sem=dma,
        oz_s=dma,
        ox_s=dma,
        oy_s=dma,
        ob_s=dma,
        oz_r=dma((NZ,)),
        ox_r=dma((3, 5)),
        oy_r=dma((NX, len(Y_GROUPS))),
        ob_r=dma((2, NX)),
        x_s=dma((2,)),
        x_r=dma((2, 8)),
        xy_s=dma,
        xy_r=dma((8,)),
        xz_s=dma((2,)),
        xz_r=dma((4,)),
        z_s=dma((2,)),
        z_r=dma((4, 4)),
        zy_s=dma,
        zy_r=dma((4,)),
        zx_s=dma((2,)),
        zx_r=dma((2,)),
        gy_s=dma,
        gy_r=dma((4,)),
        gx_s=dma,
        gx_r=dma,
        gz_s=dma,
        gz_r=dma,
        hz_s=dma,
        hz_r=dma,
        hx_s=dma,
        hx_r=dma,
        l_s=dma,
        l_r=dma,
    )
    return list(buffers), list(buffers.values())


NAMES, SHAPES = scratch()


HI = lax.Precision.HIGHEST
PANEL = 32


def factor_group(m, b):
    base = 8 * b
    tile = base // 128
    l0 = base - 128 * tile
    tiles = (0, 1, 2) if tile == 0 else (1, 2, 3)
    end = (base // PANEL + 1) * PANEL
    sub = lax.broadcasted_iota(jnp.int32, (8, 128), 0)

    def full(v):
        return jnp.broadcast_to(v, (8, 128))

    square = m[base:base+8, 128*tile:128*tile+128]
    below = [m[g:g+8, 128*tile:128*tile+128] for g in range(base+8, end, 8)]
    cols = [full(square[:, l0+k:l0+k+1]) for k in range(8)]
    e = [[full(cols[k][i:i+1]) if i >= k else None for k in range(8)] for i in range(8)]
    lower = [[full(g[:, l0+k:l0+k+1]) for k in range(8)] for g in below]
    inv = [None]*8
    for k in range(8):
        inv[k] = lax.rsqrt(e[k][k])
        for i in range(k+1, 8):
            e[i][k] = e[i][k] * inv[k]
        for i in range(k+1, 8):
            for j in range(k+1, i+1):
                e[i][j] = e[i][j] - e[i][k]*e[j][k]
    for g in lower:
        for k in range(8):
            v = g[k]
            for j in range(k):
                v = v - g[j]*e[k][j]
            g[k] = v*inv[k]
    for t in tiles:
        lanes = slice(128*t, 128*t+128)
        rows = m[base:base+8, lanes]
        u = []
        for k in range(8):
            v = full(rows[k:k+1])
            for j in range(k):
                v = v - e[k][j]*u[j]
            u.append(v*inv[k])
        o = u[0]
        for k in range(1, 8):
            o = jnp.where(sub == k, u[k], o)
        m[base:base+8, lanes] = o
        for n, g in enumerate(lower):
            r0 = base+8+8*n
            v = m[r0:r0+8, lanes]
            for k in range(8):
                v = v - g[k]*u[k]
            m[r0:r0+8, lanes] = v

def trailing(m, p):
    end = (p+1)*PANEL
    if end >= 256:
        return
    u0 = m[end-PANEL:end, :]
    for half in (0, 1):
        lo, hi = max(end, 128*half), 128*half+128
        if lo >= hi:
            continue
        first = 128*half
        last = 384 if end <= 128 else 512
        upd = lax.dot_general(u0[:, 128*half:hi], u0[:, first:last], (((0,),(0,)),((),())), precision=HI, preferred_element_type=F32)
        m[lo:hi, first:last] -= upd[lo-128*half:]


class Refs:
    pass


GATHER = (
    ("z", 1), ("z", -1), ("z", 2), ("z", -2), ("z", 3), ("z", -3), ("x", 0, 0), ("x", 0, 1), ("x", 1, 0), ("x", 1, 1),
    ("y", 0, 0), ("x", 2, 0), ("x", 2, 1), ("y", 0, 1), ("x", 0, 2), ("zp",), ("x", 3, 0), ("x", 3, 1), ("x", 1, 2),
    ("y", 1, 0), ("y", 2, 0), ("x", 4, 0), ("x", 4, 1), ("y", 0, 2), ("s", 0, 0), ("x", 2, 2), ("y", 1, 1),
    ("y", 2, 1), ("x", 3, 2), ("x", 4, 2), ("y", 1, 2), ("s", 1, 0), ("y", 2, 2), ("s", 2, 0), ("y", 3, 0),
    ("y", 3, 1), ("y", 3, 2), ("s", 3, 0), ("k", 0, 0), ("s", 0, 1), ("k", 1, 0), ("s", 1, 1), ("k", 2, 0),
    ("s", 2, 1), ("k", 3, 0), ("k", 0, 1), ("k", 1, 1), ("s", 3, 1), ("k", 2, 1), ("k", 3, 1),
)
SCHEDULE = (
    ("gl",), ("x1", 0), ("x1", 1), ("z", 0, 0), ("x1", 5), ("z", 0, 2), ("z", 0, 3), ("x1", 6), ("gx", 1),
    ("z", 0, 1), ("gx", 2), ("z", 1, 0), ("gx", 3), ("gx", 0), ("z", 1, 2), ("x1", 2), ("x1", 4), ("z", 1, 1),
    ("x1", 3), ("x1", 7), ("gz",), ("z", 2, 0), ("x2", 1), ("z", 2, 1), ("x2", 0), ("hz",), ("x2", 2), ("z", 3, 0),
    ("xf", 1), ("x2", 3), ("z", 2, 2), ("xf", 0), ("hx",), ("z", 3, 1), ("zf", 0), ("xf", 2), ("xz", 0), ("xf", 3),
    ("z", 3, 2), ("x2", 4), ("zx", 0), ("zf", 1), ("z", 1, 3), ("xz", 1), ("cs",), ("c", 2), ("x2", 5), ("c", 3),
    ("xf", 4), ("zf", 2), ("c", 3), ("x2", 6), ("z", 2, 3), ("c", 5), ("xf", 5), ("x2", 7), ("xz", 2), ("c", 4),
    ("zx", 1), ("c", 1), ("xf", 6), ("z", 3, 3), ("c", 6), ("xf", 7), ("c", 4), ("xz", 3), ("c", 3), ("zf", 3),
    ("c", 1),
)


def kernel(a_hbm, w_ref, out, *scratch_refs):
    r = Refs()
    for name, ref in zip(NAMES, scratch_refs):
        setattr(r, name, ref)
    me = lax.axis_index("blk")
    fr = lax.axis_index("freq")
    x, y, z, c = me // 16, (me // 8) % 2, me % 8, fr % 2
    d = 1 - 2 * c
    sibling = {"freq": fr + d, "blk": me}

    def at(x_, y_, z_):
        return (((x_ + 8) % 4) * 2 + y_) * 8 + (z_ + 16) % 8

    def to(x_, y_, z_):
        return {"freq": fr, "blk": at(x_, y_, z_)}

    def send(src, dst, send_sem, recv_sem, device):
        pltpu.make_async_remote_copy(
            src_ref=src,
            dst_ref=dst,
            send_sem=send_sem,
            recv_sem=recv_sem,
            device_id=device,
            device_id_type=pl.DeviceIdType.MESH,
        ).start()

    def arrived(sem, ref):
        pltpu.make_async_copy(ref, ref, sem).wait()

    copy_a = pltpu.make_async_copy(a_hbm, r.a, r.a_sem)
    copy_a.start()
    half = pl.ds(2 * c, 2)
    r.om[x, y, 0, half] = w_ref[half]

    barrier = pltpu.get_barrier_semaphore()
    across = {"freq": (fr + 2) % 4, "blk": at(x, 1 - y, z)}
    partners = [to(x + o, y, z) for o in range(1, NX)] + [to(x, y, z + o) for o in range(1, NZ)]
    partners += [to(x, 1 - y, z), across, sibling]
    for partner in partners:
        pl.semaphore_signal(barrier, inc=1, device_id=partner, device_id_type=pl.DeviceIdType.MESH)
    pl.semaphore_wait(barrier, len(partners))

    here = set()

    def need(name, *index):
        if (name, index) in here:
            return
        here.add((name, index))
        if name == "Z":
            arrived(r.oz_r.at[index[0]], r.om.at[x, y, index[0], half])
        elif name == "X":
            k, g = index
            a, b = X_GROUPS[g]
            arrived(r.ox_r.at[k, g], r.om.at[slab_x(1 + k), y, a:b, half])
        elif name == "Y":
            xi, g = index
            a, b = Y_GROUPS[g]
            arrived(r.oy_r.at[xi, g], r.om.at[slab_x(xi), 1 - y, a:b, half])
        else:
            yi, xi = index
            arrived(r.ob_r.at[yi, xi], r.om.at[slab_x(xi), y if yi == 0 else 1 - y, :, half])

    def slab_x(xi):
        return (x + (0, -d, d, 2)[xi] + 4) % 4

    def need_slab(xi, first, last):
        if xi == 0:
            for k in range(max(first, 1), last):
                need("Z", k)
        else:
            for g, (a, b) in enumerate(X_GROUPS):
                if a < last and b > first:
                    need("X", xi - 1, g)

    def z_send(oz):
        k = OFFSETS.index(-oz % NZ)
        send(r.om.at[x, y, 0, half], r.om.at[x, y, k, half], r.oz_s, r.oz_r.at[k], to(x, y, z + oz))

    def z_pass():
        need("Z", 5)
        need("Z", 6)
        send(r.om.at[x, y, 6 - c, half], r.om.at[x, y, 7, half], r.oz_s, r.oz_r.at[7], to(x, y, z + d))

    def x_send(g, k):
        a, b = X_GROUPS[g]
        need_slab(1 if k == 2 else 0, a, b)
        piece = r.om.at[slab_x(1 if k == 2 else 0), y, a:b, half]
        send(piece, piece, r.ox_s, r.ox_r.at[k, g], to(x - d if k == 1 else x + d, y, z))

    def y_send(xi, g):
        a, b = Y_GROUPS[g]
        need_slab(xi, a, b)
        for side, device in enumerate((to(x, 1 - y, z), across)):
            piece = r.om.at[slab_x(xi), y, a:b, 2 * c + side]
            send(piece, piece, r.oy_s, r.oy_r.at[xi, g], device)

    def share(xi, yi):
        if yi == 0:
            need_slab(xi, 0, NZ)
        else:
            for g in range(len(Y_GROUPS)):
                need("Y", xi, g)
        piece = r.om.at[slab_x(xi), y if yi == 0 else 1 - y, :, half]
        send(piece, piece, r.ob_s, r.ob_r.at[yi, (0, 2, 1, 3)[xi]], sibling)

    terms = []

    def sketch(xi, yi):
        if not terms:
            copy_a.wait()
        need("B", yi, xi)
        xx, yy = slab_x(xi), y if yi == 0 else 1 - y
        columns = [r.a[:, pl.ds(pl.multiple_of(at(xx, yy, z + o) * 128, 128), 128)] for o in OFFSETS]
        omega = r.om[xx, yy].reshape(1024, 256)
        value = jnp.dot(jnp.concatenate(columns, axis=1), omega, preferred_element_type=F32)
        r.acc[...] = r.acc[...] + value if terms else value
        terms.append((xi, yi))

    gather = dict(z=z_send, zp=z_pass, x=x_send, y=y_send, s=share, k=sketch)
    for name, *args in GATHER:
        gather[name](*args)

    for s in range(2):
        r.st[s] = r.acc[256 * s : 256 * s + 256].astype(BF16).astype(F32).T.astype(BF16)

    def term(pieces, block, received, out):
        columns = pl.ds(pl.multiple_of(block * 128, 128), 128)
        row = 0
        for s, k0, k1 in pieces:
            n = k1 - k0
            value = jnp.dot(r.st[s, k0:k1, :], r.a[256 * s : 256 * s + 256, columns], preferred_element_type=F32)
            for ref in received:
                value = value + ref[row : row + n, :].astype(F32)
            out[row : row + n, :] = value.astype(out.dtype)
            row += n

    def sg(way):
        return 1 - 2 * way

    def z_off(q):
        return 4 + (q // 2) * (1 - q % 2) - ((q + 1) // 2) * (q % 2)

    def x_off(q):
        return 2 - q + 3 * (q // 2) + 2 * (q // 3)

    def x_send_on(way, s, q):
        if s == 0:
            src, dst = r.xs.at[way, 0, q, way], r.xr.at[way, 0, q, way]
        else:
            src, dst = r.xs.at[way, 1, q], r.xr.at[way, 1, q]
        send(src, dst, r.x_s.at[s], r.x_r.at[s, q], to(x + sg(way), y, z))

    def x1(q):
        for way in (0, 1):
            term(X_PIECES, at(x + 2, way, z + z_off(q)), [], r.xs.at[way, 0, q, way])
            x_send_on(way, 0, q)

    def x2(q):
        arrived(r.x_r.at[0, q], r.xr.at[0, 0, q])
        for way in (0, 1):
            for yy in (0, 1):
                got = [r.xr.at[way, 0, q, way]] if yy == way else []
                term(X_PIECES, at(x + sg(way), yy, z + z_off(q)), got, r.xs.at[way, 1, q, yy])
            x_send_on(way, 1, q)

    def x_fin(q):
        arrived(r.x_r.at[1, q], r.xr.at[:, 1, q])
        for yy in (0, 1):
            got = [r.xr.at[way, 1, q, yy] for way in (0, 1)]
            term(X_PIECES, at(x, yy, z + z_off(q)), got, r.xacc.at[q, yy])
        r.xys[q] = r.xacc[q, 1 - y].astype(BF16)
        send(r.xys.at[q], r.xy.at[q], r.xy_s, r.xy_r.at[q], to(x, 1 - y, z))

    def halves(way, rows):
        return pl.ds(way * (rows // 2), rows // 2)

    def ring_step(total, sent, received, send_sem, recv_sem, s, rows, devices):
        if s:
            ring_arrived(received, recv_sem, s - 1)
        else:
            farthest = total(0)
        for way in (0, 1):
            half_rows = halves(way, rows)
            if s == 0:
                sent[way, 0, half_rows] = farthest[way * (rows // 2) : (way + 1) * (rows // 2)]
                src, dst = sent.at[way, 0, half_rows], received.at[way, 0, half_rows]
            else:
                sent[way, s] = total(2 * s - 1 + way)
                part = half_rows if s == 1 else pl.ds(0, rows)
                sent[way, s, part] += received[way, s - 1, part]
                src, dst = sent.at[way, s], received.at[way, s]
            send(src, dst, send_sem.at[min(s, 1)], recv_sem.at[s], devices[way])

    def ring_arrived(received, recv_sem, s):
        arrived(recv_sem.at[s], received.at[0, 0] if s == 0 else received.at[:, s])

    def x_total(q):
        arrived(r.xy_r.at[q], r.xy.at[q])
        return r.xacc[q, y] + r.xy[q].astype(F32)

    def xz(s):
        ring_step(x_total, r.xzs, r.xzr, r.xz_s, r.xz_r, s, KX, (to(x, y, z + 1), to(x, y, z - 1)))

    def z_arrived(s, q):
        arrived(r.z_r.at[s, q], r.zr.at[0, 0, q] if s == 0 else r.zr.at[:, s, q])

    def z_step(s, q):
        if s:
            z_arrived(s - 1, q)
        for way in (0, 1):
            far = z + sg(way) * (4 - s)
            if s == 0:
                term(Z_PIECES, at(x + x_off(q), way, far), [], r.zs.at[way, 0, q, way])
                src, dst = r.zs.at[way, 0, q, way], r.zr.at[way, 0, q, way]
            else:
                for yy in (0, 1):
                    got = [r.zr.at[way, s - 1, q, yy]] if s > 1 or yy == way else []
                    term(Z_PIECES, at(x + x_off(q), yy, far), got, r.zs.at[way, s, q, yy])
                src, dst = r.zs.at[way, s, q], r.zr.at[way, s, q]
            send(src, dst, r.z_s.at[min(s, 1)], r.z_r.at[s, q], to(x, y, z + sg(way)))

    def z_fin(q):
        z_arrived(3, q)
        for yy in (0, 1):
            got = [r.zr.at[way, 3, q, yy] for way in (0, 1)]
            term(Z_PIECES, at(x + x_off(q), yy, z), got, r.zacc.at[q, yy])
        send(r.zacc.at[q, 1 - y], r.zy.at[q], r.zy_s, r.zy_r.at[q], to(x, 1 - y, z))

    def z_total(q):
        arrived(r.zy_r.at[q], r.zy.at[q])
        return r.zacc[q, y] + r.zy[q]

    def zx(s):
        ring_step(z_total, r.zxs, r.zxr, r.zx_s, r.zx_r, s, KZ, (to(x + 1, y, z), to(x - 1, y, z)))

    def g_local():
        for s in range(2):
            value = jnp.dot(r.st[s], r.acc[256 * s : 256 * s + 256].astype(BF16), preferred_element_type=F32)
            r.gl[s] = value.reshape(4, 8, 8, 256)
        for o in (1, 2, 3, 0):
            k = (x + o) % 4
            send(r.gl.at[1 - y, k], r.gy.at[k], r.gy_s, r.gy_r.at[o], to(x, 1 - y, z))

    def g_x(o):
        k = (x + o) % 4
        arrived(r.gy_r.at[o], r.gy.at[k])
        r.gy[k] += r.gl[y, k]
        if o:
            send(r.gy.at[k], r.gx.at[o - 1], r.gx_s, r.gx_r, to(x + o, y, z))

    def g_z():
        arrived(r.gx_r, r.gx)
        r.gs[...] = r.gy[x] + r.gx[0] + r.gx[1] + r.gx[2]
        for o in range(1, NZ):
            send(r.gs.at[(z + o) % 8], r.gz.at[o - 1], r.gz_s, r.gz_r, to(x, y, z + o))

    def h_z():
        arrived(r.gz_r, r.gz)
        total = r.gs[z]
        for o in range(1, NZ):
            total = total + r.gz[o - 1]
        r.gf[x, z] = total
        piece = r.gf.at[x, z]
        for o in range(1, NZ):
            send(piece, piece, r.hz_s, r.hz_r, to(x, y, z + o))

    def h_x():
        arrived(r.hz_r, r.gf.at[x, 0:7])
        piece = r.gf.at[x]
        for o in range(1, NX):
            send(piece, piece, r.hx_s, r.hx_r, to(x + o, y, z))

    def c_start():
        arrived(r.hx_r, r.gf.at[0:3])
        r.m[:, :256] = r.gf[...].reshape(256, 256)
        row = lax.broadcasted_iota(jnp.int32, (256, 256), 0)
        column = lax.broadcasted_iota(jnp.int32, (256, 256), 1)
        r.m[:, 256:] = jnp.where(row == column, 1.0, 0.0).astype(F32)

    def c_group(b):
        factor_group(r.m, b)
        if (8 * b + 8) % PANEL == 0:
            p = 8 * b // PANEL
            trailing(r.m, p)
            rows = slice(PANEL * p, PANEL * p + PANEL)
            send(r.m.at[rows, 256:512], r.li.at[rows], r.l_s, r.l_r, to(x, 1 - y, z))

    groups = iter(range(32))

    def c_next(n):
        for b in [b for _, b in zip(range(n), groups)]:
            c_group(b)

    steps = dict(
        gl=g_local, z=z_step, x1=x1, x2=x2, gx=g_x, gz=g_z, hz=h_z, hx=h_x, xf=x_fin, zf=z_fin, xz=xz, zx=zx, cs=c_start, c=c_next
    )
    for name, *args in SCHEDULE:
        steps[name](*args)

    for pieces, total, last, received, recv_sem, ring in (
        (Z_PIECES, z_total, 3, r.zxr, r.zx_r, 2),
        (X_PIECES, x_total, 7, r.xzr, r.xz_r, 4),
    ):
        value = total(last)
        ring_arrived(received, recv_sem, ring - 1)
        value = value + received[0, ring - 1] + received[1, ring - 1]
        row = 0
        for s, k0, k1 in pieces:
            n = k1 - k0
            r.pt[s, k0:k1, :] = value[row : row + n]
            row += n

    def solved(s, inverse):
        return lax.dot_general(
            r.pt[s], inverse, (((0,), (1,)), ((), ())), precision=HI, preferred_element_type=F32
        )

    mine = solved(y, r.m[:, 256:])
    arrived(r.l_r, r.li)
    others = solved(1 - y, r.li[...])
    out[:, 0, :] = jnp.where(y == 0, mine, others)
    out[:, 1, :] = jnp.where(y == 0, others, mine)

    for sem, ref in (
        (r.oz_s, r.om.at[x, y, 0:7, half]),
        (r.ox_s, r.om.at[0:3, 0, :, half]),
        (r.oy_s, r.om.at[:, 0, :, half]),
        (r.ob_s, r.om.at[:, :, :, half]),
        (r.x_s.at[0], r.xs.at[0, 0]),
        (r.x_s.at[1], r.xs.at[:, 1]),
        (r.xy_s, r.xys),
        (r.xz_s.at[0], r.xzs.at[0, 0]),
        (r.xz_s.at[1], r.xzs.at[:, 1:4]),
        (r.z_s.at[0], r.zs.at[0, 0]),
        (r.z_s.at[1], r.zs.at[:, 1:4]),
        (r.zy_s, r.zacc.at[:, 0]),
        (r.zx_s.at[0], r.zxs.at[0, 0]),
        (r.zx_s.at[1], r.zxs.at[:, 1]),
        (r.gy_s, r.gl.at[0]),
        (r.gx_s, r.gx),
        (r.gz_s, r.gz),
        (r.hz_s, r.gz),
        (r.hx_s, r.gx),
        (r.l_s, r.li),
    ):
        arrived(sem, ref)


def local(panels, test_matrix):
    return pl.pallas_call(
        kernel,
        out_shape=jax.ShapeDtypeStruct((128, 2, 256), F32),
        in_specs=[pl.BlockSpec(memory_space=pl.ANY), pl.BlockSpec(memory_space=pltpu.VMEM)],
        out_specs=pl.BlockSpec(memory_space=pltpu.VMEM),
        scratch_shapes=SHAPES,
        compiler_params=pltpu.CompilerParams(
            collective_id=0, has_side_effects=True, vmem_limit_bytes=60 * 1024 * 1024
        ),
    )(panels.reshape(512, 8192), test_matrix.reshape(4, 32, 256))


def solution(mesh):
    in_specs = (P("freq", None, "blk", None), P("blk", None))
    out_specs = P("blk", "freq", None)
    return jax.shard_map(local, mesh=mesh, in_specs=in_specs, out_specs=out_specs, check_vma=False)
```

```python
import functools

import jax
import jax.numpy as jnp
from jax import lax
from jax.experimental import pallas as pl
from jax.experimental.pallas import tpu as pltpu
from jax.sharding import PartitionSpec as P

F32 = jnp.float32
BF16 = jnp.bfloat16
NX, NY, NZ = 4, 2, 8
X_PIECES = ((0, 0, 256), (1, 0, 32))
Z_PIECES = ((1, 32, 256),)
OFFSETS = (0, 1, 7, 2, 6, 3, 5, 4)
X_GROUPS = ((0, 1), (1, 3), (3, 5), (5, 7), (7, 8))
Y_GROUPS = ((0, 3), (3, 5), (5, 8))
KX = sum(k1 - k0 for _, k0, k1 in X_PIECES)
KZ = sum(k1 - k0 for _, k0, k1 in Z_PIECES)


def scratch():
    dma = pltpu.SemaphoreType.DMA
    buffers = dict(
        om=pltpu.VMEM((NX, NY, NZ, 4, 32, 256), BF16),
        a=pltpu.VMEM((512, 8192), BF16),
        acc=pltpu.VMEM((512, 256), F32),
        st=pltpu.VMEM((2, 256, 256), BF16),
        xs=pltpu.VMEM((2, 2, 8, 2, KX, 128), BF16),
        xr=pltpu.VMEM((2, 2, 8, 2, KX, 128), BF16),
        xacc=pltpu.VMEM((8, 2, KX, 128), F32),
        xys=pltpu.VMEM((8, KX, 128), BF16),
        xy=pltpu.VMEM((8, KX, 128), BF16),
        xzs=pltpu.VMEM((2, 4, KX, 128), F32),
        xzr=pltpu.VMEM((2, 4, KX, 128), F32),
        zs=pltpu.VMEM((2, 4, 4, 2, KZ, 128), BF16),
        zr=pltpu.VMEM((2, 4, 4, 2, KZ, 128), BF16),
        zacc=pltpu.VMEM((4, 2, KZ, 128), F32),
        zy=pltpu.VMEM((4, KZ, 128), F32),
        zxs=pltpu.VMEM((2, 2, KZ, 128), F32),
        zxr=pltpu.VMEM((2, 2, KZ, 128), F32),
        gl=pltpu.VMEM((2, 4, 8, 8, 256), F32),
        gy=pltpu.VMEM((4, 8, 8, 256), F32),
        gx=pltpu.VMEM((3, 8, 8, 256), F32),
        gs=pltpu.VMEM((8, 8, 256), F32),
        gz=pltpu.VMEM((7, 8, 256), F32),
        gf=pltpu.VMEM((4, 8, 8, 256), F32),
        m=pltpu.VMEM((256, 512), F32),
        li=pltpu.VMEM((256, 256), F32),
        pt=pltpu.VMEM((2, 256, 128), F32),
        a_sem=dma,
        oz_s=dma,
        ox_s=dma,
        oy_s=dma,
        ob_s=dma,
        oz_r=dma((NZ,)),
        ox_r=dma((3, 5)),
        oy_r=dma((NX, len(Y_GROUPS))),
        ob_r=dma((2, NX)),
        x_s=dma((2,)),
        x_r=dma((2, 8)),
        xy_s=dma,
        xy_r=dma((8,)),
        xz_s=dma((2,)),
        xz_r=dma((4,)),
        z_s=dma((2,)),
        z_r=dma((4, 4)),
        zy_s=dma,
        zy_r=dma((4,)),
        zx_s=dma((2,)),
        zx_r=dma((2,)),
        gy_s=dma,
        gy_r=dma((4,)),
        gx_s=dma,
        gx_r=dma,
        gz_s=dma,
        gz_r=dma,
        hz_s=dma,
        hz_r=dma,
        hx_s=dma,
        hx_r=dma,
        l_s=dma,
        l_r=dma,
    )
    return list(buffers), list(buffers.values())


NAMES, SHAPES = scratch()


HI = lax.Precision.HIGHEST
PANEL = 32


def factor_group(m, b):
    base = 8 * b
    tile = base // 128
    l0 = base - 128 * tile
    tiles = (0, 1, 2) if tile == 0 else (1, 2, 3)
    end = (base // PANEL + 1) * PANEL
    sub = lax.broadcasted_iota(jnp.int32, (8, 128), 0)

    def full(v):
        return jnp.broadcast_to(v, (8, 128))

    square = m[base:base+8, 128*tile:128*tile+128]
    below = [m[g:g+8, 128*tile:128*tile+128] for g in range(base+8, end, 8)]
    cols = [full(square[:, l0+k:l0+k+1]) for k in range(8)]
    e = [[full(cols[k][i:i+1]) if i >= k else None for k in range(8)] for i in range(8)]
    lower = [[full(g[:, l0+k:l0+k+1]) for k in range(8)] for g in below]
    inv = [None]*8
    for k in range(8):
        inv[k] = lax.rsqrt(e[k][k])
        for i in range(k+1, 8):
            e[i][k] = e[i][k] * inv[k]
        for i in range(k+1, 8):
            for j in range(k+1, i+1):
                e[i][j] = e[i][j] - e[i][k]*e[j][k]
    for g in lower:
        for k in range(8):
            v = g[k]
            for j in range(k):
                v = v - g[j]*e[k][j]
            g[k] = v*inv[k]
    for t in tiles:
        lanes = slice(128*t, 128*t+128)
        rows = m[base:base+8, lanes]
        u = []
        for k in range(8):
            v = full(rows[k:k+1])
            for j in range(k):
                v = v - e[k][j]*u[j]
            u.append(v*inv[k])
        o = u[0]
        for k in range(1, 8):
            o = jnp.where(sub == k, u[k], o)
        m[base:base+8, lanes] = o
        for n, g in enumerate(lower):
            r0 = base+8+8*n
            v = m[r0:r0+8, lanes]
            for k in range(8):
                v = v - g[k]*u[k]
            m[r0:r0+8, lanes] = v

def trailing(m, p):
    end = (p+1)*PANEL
    if end >= 256:
        return
    u0 = m[end-PANEL:end, :]
    for half in (0, 1):
        lo, hi = max(end, 128*half), 128*half+128
        if lo >= hi:
            continue
        first = 128*half
        last = 384 if end <= 128 else 512
        upd = lax.dot_general(u0[:, 128*half:hi], u0[:, first:last], (((0,),(0,)),((),())), precision=HI, preferred_element_type=F32)
        m[lo:hi, first:last] -= upd[lo-128*half:]


class Refs:
    pass


GATHER = (
    ("x", 0, 0), ("x", 0, 1), ("z", 1), ("z", -1), ("z", 2), ("z", -2), ("z", 3), ("z", -3), ("z", 4), ("x", 1, 0),
    ("x", 1, 1), ("y", 0, 0), ("x", 2, 0), ("x", 2, 1), ("y", 0, 1), ("x", 0, 2), ("x", 3, 0), ("x", 3, 1),
    ("x", 1, 2), ("y", 1, 0), ("y", 2, 0), ("x", 4, 0), ("x", 4, 1), ("y", 0, 2), ("s", 0, 0), ("x", 2, 2),
    ("y", 1, 1), ("y", 2, 1), ("x", 3, 2), ("x", 4, 2), ("y", 1, 2), ("s", 1, 0), ("y", 2, 2), ("s", 2, 0),
    ("y", 3, 0), ("y", 3, 1), ("y", 3, 2), ("s", 3, 0), ("k", 0, 0), ("s", 0, 1), ("k", 1, 0), ("s", 1, 1),
    ("k", 2, 0), ("s", 2, 1), ("k", 3, 0), ("k", 0, 1), ("k", 1, 1), ("s", 3, 1), ("k", 2, 1), ("k", 3, 1),
)
SCHEDULE = (
    ("x1", 5), ("z", 0, 2), ("x1", 3), ("z", 0, 1), ("gl",), ("x1", 4), ("z", 0, 0), ("z", 0, 3), ("z", 1, 2),
    ("x1", 1), ("gx", 1), ("gx", 2), ("z", 1, 0), ("z", 1, 3), ("x1", 0), ("gx", 3), ("x2", 3), ("x1", 2),
    ("z", 2, 2), ("gx", 0), ("x2", 1), ("gz",), ("x2", 0), ("z", 1, 1), ("z", 2, 0), ("x2", 2), ("hz",), ("xf", 1),
    ("z", 2, 1), ("z", 3, 2), ("z", 3, 0), ("x1", 6), ("xf", 3), ("hx",), ("xf", 0), ("z", 3, 1), ("xf", 2),
    ("x2", 4), ("zf", 2), ("xz", 0), ("zf", 0), ("x2", 5), ("x2", 6), ("z", 2, 3), ("cs",), ("c", 1), ("zf", 1),
    ("c", 2), ("x1", 7), ("c", 1), ("xz", 1), ("c", 1), ("xf", 4), ("c", 8), ("z", 3, 3), ("c", 2), ("xf", 5),
    ("c", 2), ("zx", 0), ("xz", 2), ("c", 1), ("xf", 6), ("c", 3), ("x2", 7), ("c", 3), ("zf", 3), ("zx", 1),
    ("c", 5), ("xz", 3), ("c", 3), ("xf", 7),
)


def kernel(a_hbm, w_ref, out, *scratch_refs):
    r = Refs()
    for name, ref in zip(NAMES, scratch_refs):
        setattr(r, name, ref)
    me = lax.axis_index("blk")
    fr = lax.axis_index("freq")
    x, y, z, c = me // 16, (me // 8) % 2, me % 8, fr % 2
    d = 1 - 2 * c
    sibling = {"freq": fr + d, "blk": me}

    def at(x_, y_, z_):
        return (((x_ + 8) % 4) * 2 + y_) * 8 + (z_ + 16) % 8

    def to(x_, y_, z_):
        return {"freq": fr, "blk": at(x_, y_, z_)}

    def send(src, dst, send_sem, recv_sem, device):
        pltpu.make_async_remote_copy(
            src_ref=src,
            dst_ref=dst,
            send_sem=send_sem,
            recv_sem=recv_sem,
            device_id=device,
            device_id_type=pl.DeviceIdType.MESH,
        ).start()

    def arrived(sem, ref):
        pltpu.make_async_copy(ref, ref, sem).wait()

    copy_a = pltpu.make_async_copy(a_hbm, r.a, r.a_sem)
    copy_a.start()
    half = pl.ds(2 * c, 2)
    r.om[x, y, 0, half] = w_ref[half]

    barrier = pltpu.get_barrier_semaphore()
    across = {"freq": (fr + 2) % 4, "blk": at(x, 1 - y, z)}
    partners = [to(x + o, y, z) for o in range(1, NX)] + [to(x, y, z + o) for o in range(1, NZ)]
    partners += [to(x, 1 - y, z), across, sibling]
    for partner in partners:
        pl.semaphore_signal(barrier, inc=1, device_id=partner, device_id_type=pl.DeviceIdType.MESH)
    pl.semaphore_wait(barrier, len(partners))

    here = set()

    def need(name, *index):
        if (name, index) in here:
            return
        here.add((name, index))
        if name == "Z":
            arrived(r.oz_r.at[index[0]], r.om.at[x, y, index[0], half])
        elif name == "X":
            k, g = index
            a, b = X_GROUPS[g]
            arrived(r.ox_r.at[k, g], r.om.at[slab_x(1 + k), y, a:b, half])
        elif name == "Y":
            xi, g = index
            a, b = Y_GROUPS[g]
            arrived(r.oy_r.at[xi, g], r.om.at[slab_x(xi), 1 - y, a:b, half])
        else:
            yi, xi = index
            arrived(r.ob_r.at[yi, xi], r.om.at[slab_x(xi), y if yi == 0 else 1 - y, :, half])

    def slab_x(xi):
        return (x + (0, -d, d, 2)[xi] + 4) % 4

    def need_slab(xi, first, last):
        if xi == 0:
            for k in range(max(first, 1), last):
                need("Z", k)
        else:
            for g, (a, b) in enumerate(X_GROUPS):
                if a < last and b > first:
                    need("X", xi - 1, g)

    def z_send(oz):
        k = OFFSETS.index(-oz % NZ)
        send(r.om.at[x, y, 0, half], r.om.at[x, y, k, half], r.oz_s, r.oz_r.at[k], to(x, y, z + oz))

    def z_pass():
        need("Z", 5)
        need("Z", 6)
        send(r.om.at[x, y, 6 - c, half], r.om.at[x, y, 7, half], r.oz_s, r.oz_r.at[7], to(x, y, z + d))

    def x_send(g, k):
        a, b = X_GROUPS[g]
        need_slab(1 if k == 2 else 0, a, b)
        piece = r.om.at[slab_x(1 if k == 2 else 0), y, a:b, half]
        send(piece, piece, r.ox_s, r.ox_r.at[k, g], to(x - d if k == 1 else x + d, y, z))

    def y_send(xi, g):
        a, b = Y_GROUPS[g]
        need_slab(xi, a, b)
        for side, device in enumerate((to(x, 1 - y, z), across)):
            piece = r.om.at[slab_x(xi), y, a:b, 2 * c + side]
            send(piece, piece, r.oy_s, r.oy_r.at[xi, g], device)

    def share(xi, yi):
        if yi == 0:
            need_slab(xi, 0, NZ)
        else:
            for g in range(len(Y_GROUPS)):
                need("Y", xi, g)
        piece = r.om.at[slab_x(xi), y if yi == 0 else 1 - y, :, half]
        send(piece, piece, r.ob_s, r.ob_r.at[yi, (0, 2, 1, 3)[xi]], sibling)

    terms = []

    def sketch(xi, yi):
        if not terms:
            copy_a.wait()
        need("B", yi, xi)
        xx, yy = slab_x(xi), y if yi == 0 else 1 - y
        columns = [r.a[:, pl.ds(pl.multiple_of(at(xx, yy, z + o) * 128, 128), 128)] for o in OFFSETS]
        omega = r.om[xx, yy].reshape(1024, 256)
        value = jnp.dot(jnp.concatenate(columns, axis=1), omega, preferred_element_type=F32)
        r.acc[...] = r.acc[...] + value if terms else value
        terms.append((xi, yi))

    gather = dict(z=z_send, zp=z_pass, x=x_send, y=y_send, s=share, k=sketch)
    for name, *args in GATHER:
        gather[name](*args)

    for s in range(2):
        r.st[s] = r.acc[256 * s : 256 * s + 256].astype(BF16).astype(F32).T.astype(BF16)

    def term(pieces, block, received, out):
        columns = pl.ds(pl.multiple_of(block * 128, 128), 128)
        row = 0
        for s, k0, k1 in pieces:
            n = k1 - k0
            value = jnp.dot(r.st[s, k0:k1, :], r.a[256 * s : 256 * s + 256, columns], preferred_element_type=F32)
            for ref in received:
                value = value + ref[row : row + n, :].astype(F32)
            out[row : row + n, :] = value.astype(out.dtype)
            row += n

    def sg(way):
        return 1 - 2 * way

    def z_off(q):
        return 4 + (q // 2) * (1 - q % 2) - ((q + 1) // 2) * (q % 2)

    def x_off(q):
        return 2 - q + 3 * (q // 2) + 2 * (q // 3)

    def x_send_on(way, s, q):
        if s == 0:
            src, dst = r.xs.at[way, 0, q, way], r.xr.at[way, 0, q, way]
        else:
            src, dst = r.xs.at[way, 1, q], r.xr.at[way, 1, q]
        send(src, dst, r.x_s.at[s], r.x_r.at[s, q], to(x + sg(way), y, z))

    def x1(q):
        for way in (0, 1):
            term(X_PIECES, at(x + 2, way, z + z_off(q)), [], r.xs.at[way, 0, q, way])
            x_send_on(way, 0, q)

    def x2(q):
        arrived(r.x_r.at[0, q], r.xr.at[0, 0, q])
        for way in (0, 1):
            for yy in (0, 1):
                got = [r.xr.at[way, 0, q, way]] if yy == way else []
                term(X_PIECES, at(x + sg(way), yy, z + z_off(q)), got, r.xs.at[way, 1, q, yy])
            x_send_on(way, 1, q)

    def x_fin(q):
        arrived(r.x_r.at[1, q], r.xr.at[:, 1, q])
        for yy in (0, 1):
            got = [r.xr.at[way, 1, q, yy] for way in (0, 1)]
            term(X_PIECES, at(x, yy, z + z_off(q)), got, r.xacc.at[q, yy])
        r.xys[q] = r.xacc[q, 1 - y].astype(BF16)
        send(r.xys.at[q], r.xy.at[q], r.xy_s, r.xy_r.at[q], to(x, 1 - y, z))

    def halves(way, rows):
        return pl.ds(way * (rows // 2), rows // 2)

    def ring_step(total, sent, received, send_sem, recv_sem, s, rows, devices):
        if s:
            ring_arrived(received, recv_sem, s - 1)
        else:
            farthest = total(0)
        for way in (0, 1):
            half_rows = halves(way, rows)
            if s == 0:
                sent[way, 0, half_rows] = farthest[way * (rows // 2) : (way + 1) * (rows // 2)]
                src, dst = sent.at[way, 0, half_rows], received.at[way, 0, half_rows]
            else:
                sent[way, s] = total(2 * s - 1 + way)
                part = half_rows if s == 1 else pl.ds(0, rows)
                sent[way, s, part] += received[way, s - 1, part]
                src, dst = sent.at[way, s], received.at[way, s]
            send(src, dst, send_sem.at[min(s, 1)], recv_sem.at[s], devices[way])

    def ring_arrived(received, recv_sem, s):
        arrived(recv_sem.at[s], received.at[0, 0] if s == 0 else received.at[:, s])

    def x_total(q):
        arrived(r.xy_r.at[q], r.xy.at[q])
        return r.xacc[q, y] + r.xy[q].astype(F32)

    def xz(s):
        ring_step(x_total, r.xzs, r.xzr, r.xz_s, r.xz_r, s, KX, (to(x, y, z + 1), to(x, y, z - 1)))

    def z_arrived(s, q):
        arrived(r.z_r.at[s, q], r.zr.at[0, 0, q] if s == 0 else r.zr.at[:, s, q])

    def z_step(s, q):
        if s:
            z_arrived(s - 1, q)
        for way in (0, 1):
            far = z + sg(way) * (4 - s)
            if s == 0:
                term(Z_PIECES, at(x + x_off(q), way, far), [], r.zs.at[way, 0, q, way])
                src, dst = r.zs.at[way, 0, q, way], r.zr.at[way, 0, q, way]
            else:
                for yy in (0, 1):
                    got = [r.zr.at[way, s - 1, q, yy]] if s > 1 or yy == way else []
                    term(Z_PIECES, at(x + x_off(q), yy, far), got, r.zs.at[way, s, q, yy])
                src, dst = r.zs.at[way, s, q], r.zr.at[way, s, q]
            send(src, dst, r.z_s.at[min(s, 1)], r.z_r.at[s, q], to(x, y, z + sg(way)))

    def z_fin(q):
        z_arrived(3, q)
        for yy in (0, 1):
            got = [r.zr.at[way, 3, q, yy] for way in (0, 1)]
            term(Z_PIECES, at(x + x_off(q), yy, z), got, r.zacc.at[q, yy])
        send(r.zacc.at[q, 1 - y], r.zy.at[q], r.zy_s, r.zy_r.at[q], to(x, 1 - y, z))

    def z_total(q):
        arrived(r.zy_r.at[q], r.zy.at[q])
        return r.zacc[q, y] + r.zy[q]

    def zx(s):
        ring_step(z_total, r.zxs, r.zxr, r.zx_s, r.zx_r, s, KZ, (to(x + 1, y, z), to(x - 1, y, z)))

    def g_local():
        for s in range(2):
            value = jnp.dot(r.st[s], r.acc[256 * s : 256 * s + 256].astype(BF16), preferred_element_type=F32)
            r.gl[s] = value.reshape(4, 8, 8, 256)
        for o in (1, 2, 3, 0):
            k = (x + o) % 4
            send(r.gl.at[1 - y, k], r.gy.at[k], r.gy_s, r.gy_r.at[o], to(x, 1 - y, z))

    def g_x(o):
        k = (x + o) % 4
        arrived(r.gy_r.at[o], r.gy.at[k])
        r.gy[k] += r.gl[y, k]
        if o:
            send(r.gy.at[k], r.gx.at[o - 1], r.gx_s, r.gx_r, to(x + o, y, z))

    def g_z():
        arrived(r.gx_r, r.gx)
        r.gs[...] = r.gy[x] + r.gx[0] + r.gx[1] + r.gx[2]
        for o in range(1, NZ):
            send(r.gs.at[(z + o) % 8], r.gz.at[o - 1], r.gz_s, r.gz_r, to(x, y, z + o))

    def h_z():
        arrived(r.gz_r, r.gz)
        total = r.gs[z]
        for o in range(1, NZ):
            total = total + r.gz[o - 1]
        r.gf[x, z] = total
        piece = r.gf.at[x, z]
        for o in range(1, NZ):
            send(piece, piece, r.hz_s, r.hz_r, to(x, y, z + o))

    def h_x():
        arrived(r.hz_r, r.gf.at[x, 0:7])
        piece = r.gf.at[x]
        for o in range(1, NX):
            send(piece, piece, r.hx_s, r.hx_r, to(x + o, y, z))

    def c_start():
        arrived(r.hx_r, r.gf.at[0:3])
        r.m[:, :256] = r.gf[...].reshape(256, 256)
        row = lax.broadcasted_iota(jnp.int32, (256, 256), 0)
        column = lax.broadcasted_iota(jnp.int32, (256, 256), 1)
        r.m[:, 256:] = jnp.where(row == column, 1.0, 0.0).astype(F32)

    def c_group(b):
        factor_group(r.m, b)
        if (8 * b + 8) % PANEL == 0:
            p = 8 * b // PANEL
            trailing(r.m, p)
            rows = slice(PANEL * p, PANEL * p + PANEL)
            send(r.m.at[rows, 256:512], r.li.at[rows], r.l_s, r.l_r, to(x, 1 - y, z))

    groups = iter(range(32))

    def c_next(n):
        for b in [b for _, b in zip(range(n), groups)]:
            c_group(b)

    steps = dict(
        gl=g_local, z=z_step, x1=x1, x2=x2, gx=g_x, gz=g_z, hz=h_z, hx=h_x, xf=x_fin, zf=z_fin, xz=xz, zx=zx, cs=c_start, c=c_next
    )
    for name, *args in SCHEDULE:
        steps[name](*args)

    for pieces, total, last, received, recv_sem, ring in (
        (Z_PIECES, z_total, 3, r.zxr, r.zx_r, 2),
        (X_PIECES, x_total, 7, r.xzr, r.xz_r, 4),
    ):
        value = total(last)
        ring_arrived(received, recv_sem, ring - 1)
        value = value + received[0, ring - 1] + received[1, ring - 1]
        row = 0
        for s, k0, k1 in pieces:
            n = k1 - k0
            r.pt[s, k0:k1, :] = value[row : row + n]
            row += n

    def solved(s, inverse):
        return lax.dot_general(
            r.pt[s], inverse, (((0,), (1,)), ((), ())), precision=HI, preferred_element_type=F32
        )

    mine = solved(y, r.m[:, 256:])
    arrived(r.l_r, r.li)
    others = solved(1 - y, r.li[...])
    out[:, 0, :] = jnp.where(y == 0, mine, others)
    out[:, 1, :] = jnp.where(y == 0, others, mine)

    for sem, ref in (
        (r.oz_s, r.om.at[x, y, 0:7, half]),
        (r.ox_s, r.om.at[0:3, 0, :, half]),
        (r.oy_s, r.om.at[:, 0, :, half]),
        (r.ob_s, r.om.at[:, :, :, half]),
        (r.x_s.at[0], r.xs.at[0, 0]),
        (r.x_s.at[1], r.xs.at[:, 1]),
        (r.xy_s, r.xys),
        (r.xz_s.at[0], r.xzs.at[0, 0]),
        (r.xz_s.at[1], r.xzs.at[:, 1:4]),
        (r.z_s.at[0], r.zs.at[0, 0]),
        (r.z_s.at[1], r.zs.at[:, 1:4]),
        (r.zy_s, r.zacc.at[:, 0]),
        (r.zx_s.at[0], r.zxs.at[0, 0]),
        (r.zx_s.at[1], r.zxs.at[:, 1]),
        (r.gy_s, r.gl.at[0]),
        (r.gx_s, r.gx),
        (r.gz_s, r.gz),
        (r.hz_s, r.gz),
        (r.hx_s, r.gx),
        (r.l_s, r.li),
    ):
        arrived(sem, ref)


def local(panels, test_matrix):
    return pl.pallas_call(
        kernel,
        out_shape=jax.ShapeDtypeStruct((128, 2, 256), F32),
        in_specs=[pl.BlockSpec(memory_space=pl.ANY), pl.BlockSpec(memory_space=pltpu.VMEM)],
        out_specs=pl.BlockSpec(memory_space=pltpu.VMEM),
        scratch_shapes=SHAPES,
        compiler_params=pltpu.CompilerParams(
            collective_id=0, has_side_effects=True, vmem_limit_bytes=60 * 1024 * 1024
        ),
    )(panels.reshape(512, 8192), test_matrix.reshape(4, 32, 256))


def solution(mesh):
    in_specs = (P("freq", None, "blk", None), P("blk", None))
    out_specs = P("blk", "freq", None)
    return jax.shard_map(local, mesh=mesh, in_specs=in_specs, out_specs=out_specs, check_vma=False)
```

```python
import functools

import jax
import jax.numpy as jnp
from jax import lax
from jax.experimental import pallas as pl
from jax.experimental.pallas import tpu as pltpu
from jax.sharding import PartitionSpec as P

F32 = jnp.float32
BF16 = jnp.bfloat16
NX, NY, NZ = 4, 2, 8
X_PIECES = ((0, 0, 256), (1, 0, 32))
Z_PIECES = ((1, 32, 256),)
OFFSETS = (0, 1, 7, 2, 6, 3, 5, 4)
X_GROUPS = ((0, 1), (1, 3), (3, 5), (5, 7), (7, 8))
Y_GROUPS = ((0, 3), (3, 5), (5, 8))
KX = sum(k1 - k0 for _, k0, k1 in X_PIECES)
KZ = sum(k1 - k0 for _, k0, k1 in Z_PIECES)


def scratch():
    dma = pltpu.SemaphoreType.DMA
    buffers = dict(
        om=pltpu.VMEM((NX, NY, NZ, 4, 32, 256), BF16),
        a=pltpu.VMEM((512, 8192), BF16),
        acc=pltpu.VMEM((512, 256), F32),
        st=pltpu.VMEM((2, 256, 256), BF16),
        xs=pltpu.VMEM((2, 2, 8, 2, KX, 128), BF16),
        xr=pltpu.VMEM((2, 2, 8, 2, KX, 128), BF16),
        xacc=pltpu.VMEM((8, 2, KX, 128), F32),
        xys=pltpu.VMEM((8, KX, 128), BF16),
        xy=pltpu.VMEM((8, KX, 128), BF16),
        xzs=pltpu.VMEM((2, 4, KX, 128), F32),
        xzr=pltpu.VMEM((2, 4, KX, 128), F32),
        zs=pltpu.VMEM((2, 4, 4, 2, KZ, 128), BF16),
        zr=pltpu.VMEM((2, 4, 4, 2, KZ, 128), BF16),
        zacc=pltpu.VMEM((4, 2, KZ, 128), F32),
        zy=pltpu.VMEM((4, KZ, 128), F32),
        zxs=pltpu.VMEM((2, 2, KZ, 128), F32),
        zxr=pltpu.VMEM((2, 2, KZ, 128), F32),
        gl=pltpu.VMEM((2, 4, 8, 8, 256), F32),
        gy=pltpu.VMEM((4, 8, 8, 256), F32),
        gx=pltpu.VMEM((3, 8, 8, 256), F32),
        gs=pltpu.VMEM((8, 8, 256), F32),
        gz=pltpu.VMEM((7, 8, 256), F32),
        gf=pltpu.VMEM((4, 8, 8, 256), F32),
        m=pltpu.VMEM((256, 512), F32),
        li=pltpu.VMEM((256, 256), F32),
        pt=pltpu.VMEM((2, 256, 128), F32),
        a_sem=dma,
        oz_s=dma,
        ox_s=dma,
        oy_s=dma,
        ob_s=dma,
        oz_r=dma((NZ,)),
        ox_r=dma((3, 5)),
        oy_r=dma((NX, len(Y_GROUPS))),
        ob_r=dma((2, NX)),
        x_s=dma((2,)),
        x_r=dma((2, 8)),
        xy_s=dma,
        xy_r=dma((8,)),
        xz_s=dma((2,)),
        xz_r=dma((4,)),
        z_s=dma((2,)),
        z_r=dma((4, 4)),
        zy_s=dma,
        zy_r=dma((4,)),
        zx_s=dma((2,)),
        zx_r=dma((2,)),
        gy_s=dma,
        gy_r=dma((4,)),
        gx_s=dma,
        gx_r=dma,
        gz_s=dma,
        gz_r=dma,
        hz_s=dma,
        hz_r=dma,
        hx_s=dma,
        hx_r=dma,
        l_s=dma,
        l_r=dma,
    )
    return list(buffers), list(buffers.values())


NAMES, SHAPES = scratch()


HI = lax.Precision.HIGHEST
PANEL = 32


def factor_group(m, b):
    base = 8 * b
    tile = base // 128
    l0 = base - 128 * tile
    tiles = (0, 1, 2) if tile == 0 else (1, 2, 3)
    end = (base // PANEL + 1) * PANEL
    sub = lax.broadcasted_iota(jnp.int32, (8, 128), 0)

    def full(v):
        return jnp.broadcast_to(v, (8, 128))

    square = m[base:base+8, 128*tile:128*tile+128]
    below = [m[g:g+8, 128*tile:128*tile+128] for g in range(base+8, end, 8)]
    cols = [full(square[:, l0+k:l0+k+1]) for k in range(8)]
    e = [[full(cols[k][i:i+1]) if i >= k else None for k in range(8)] for i in range(8)]
    lower = [[full(g[:, l0+k:l0+k+1]) for k in range(8)] for g in below]
    inv = [None]*8
    for k in range(8):
        inv[k] = lax.rsqrt(e[k][k])
        for i in range(k+1, 8):
            e[i][k] = e[i][k] * inv[k]
        for i in range(k+1, 8):
            for j in range(k+1, i+1):
                e[i][j] = e[i][j] - e[i][k]*e[j][k]
    for g in lower:
        for k in range(8):
            v = g[k]
            for j in range(k):
                v = v - g[j]*e[k][j]
            g[k] = v*inv[k]
    for t in tiles:
        lanes = slice(128*t, 128*t+128)
        rows = m[base:base+8, lanes]
        u = []
        for k in range(8):
            v = full(rows[k:k+1])
            for j in range(k):
                v = v - e[k][j]*u[j]
            u.append(v*inv[k])
        o = u[0]
        for k in range(1, 8):
            o = jnp.where(sub == k, u[k], o)
        m[base:base+8, lanes] = o
        for n, g in enumerate(lower):
            r0 = base+8+8*n
            v = m[r0:r0+8, lanes]
            for k in range(8):
                v = v - g[k]*u[k]
            m[r0:r0+8, lanes] = v

def trailing(m, p):
    end = (p+1)*PANEL
    if end >= 256:
        return
    u0 = m[end-PANEL:end, :]
    for half in (0, 1):
        lo, hi = max(end, 128*half), 128*half+128
        if lo >= hi:
            continue
        first = 128*half
        last = 384 if end <= 128 else 512
        upd = lax.dot_general(u0[:, 128*half:hi], u0[:, first:last], (((0,),(0,)),((),())), precision=HI, preferred_element_type=F32)
        m[lo:hi, first:last] -= upd[lo-128*half:]


class Refs:
    pass


GATHER = (
    ("x", 0, 0), ("x", 0, 1), ("z", 1), ("z", -1), ("z", 2), ("z", -2), ("z", 3), ("z", -3), ("z", 4), ("x", 1, 0),
    ("x", 1, 1), ("y", 0, 0), ("x", 2, 0), ("x", 2, 1), ("y", 0, 1), ("x", 0, 2), ("x", 3, 0), ("x", 3, 1),
    ("x", 1, 2), ("y", 1, 0), ("y", 2, 0), ("x", 4, 0), ("x", 4, 1), ("y", 0, 2), ("s", 0, 0), ("x", 2, 2),
    ("y", 1, 1), ("y", 2, 1), ("x", 3, 2), ("x", 4, 2), ("y", 1, 2), ("s", 1, 0), ("y", 2, 2), ("s", 2, 0),
    ("y", 3, 0), ("y", 3, 1), ("y", 3, 2), ("s", 3, 0), ("k", 0, 0), ("s", 0, 1), ("k", 1, 0), ("s", 1, 1),
    ("k", 2, 0), ("s", 2, 1), ("k", 3, 0), ("k", 0, 1), ("k", 1, 1), ("s", 3, 1), ("k", 2, 1), ("k", 3, 1),
)
SCHEDULE = (
    ("x1", 1), ("z", 0, 1), ("x1", 3), ("z", 0, 2), ("gl",), ("z", 0, 3), ("z", 0, 0), ("x1", 2), ("x1", 6),
    ("z", 1, 1), ("z", 1, 2), ("gx", 1), ("gx", 2), ("gx", 3), ("x1", 0), ("z", 1, 0), ("x2", 1), ("z", 2, 1),
    ("gx", 0), ("gz",), ("x2", 0), ("x2", 2), ("z", 2, 0), ("z", 2, 2), ("x1", 4), ("x2", 3), ("xf", 0), ("hz",),
    ("z", 3, 0), ("z", 3, 1), ("z", 1, 3), ("z", 3, 2), ("xz", 0), ("x1", 5), ("xf", 2), ("xf", 1), ("hx",),
    ("zf", 0), ("x2", 4), ("x2", 5), ("x2", 6), ("xf", 3), ("zf", 1), ("x1", 7), ("zx", 0), ("z", 2, 3), ("cs",),
    ("zf", 2), ("c", 4), ("xz", 1), ("c", 2), ("xf", 4), ("c", 7), ("z", 3, 3), ("xf", 5), ("c", 5), ("xz", 2),
    ("c", 1), ("xf", 6), ("c", 3), ("x2", 7), ("c", 1), ("zf", 3), ("c", 1), ("zx", 1), ("c", 5), ("xz", 3), ("c", 3),
    ("xf", 7),
)


def kernel(a_hbm, w_ref, out, *scratch_refs):
    r = Refs()
    for name, ref in zip(NAMES, scratch_refs):
        setattr(r, name, ref)
    me = lax.axis_index("blk")
    fr = lax.axis_index("freq")
    x, y, z, c = me // 16, (me // 8) % 2, me % 8, fr % 2
    d = 1 - 2 * c
    sibling = {"freq": fr + d, "blk": me}

    def at(x_, y_, z_):
        return (((x_ + 8) % 4) * 2 + y_) * 8 + (z_ + 16) % 8

    def to(x_, y_, z_):
        return {"freq": fr, "blk": at(x_, y_, z_)}

    def send(src, dst, send_sem, recv_sem, device):
        pltpu.make_async_remote_copy(
            src_ref=src,
            dst_ref=dst,
            send_sem=send_sem,
            recv_sem=recv_sem,
            device_id=device,
            device_id_type=pl.DeviceIdType.MESH,
        ).start()

    def arrived(sem, ref):
        pltpu.make_async_copy(ref, ref, sem).wait()

    copy_a = pltpu.make_async_copy(a_hbm, r.a, r.a_sem)
    copy_a.start()
    half = pl.ds(2 * c, 2)
    r.om[x, y, 0, half] = w_ref[half]

    barrier = pltpu.get_barrier_semaphore()
    across = {"freq": (fr + 2) % 4, "blk": at(x, 1 - y, z)}
    partners = [to(x + o, y, z) for o in range(1, NX)] + [to(x, y, z + o) for o in range(1, NZ)]
    partners += [to(x, 1 - y, z), across, sibling]
    for partner in partners:
        pl.semaphore_signal(barrier, inc=1, device_id=partner, device_id_type=pl.DeviceIdType.MESH)
    pl.semaphore_wait(barrier, len(partners))

    here = set()

    def need(name, *index):
        if (name, index) in here:
            return
        here.add((name, index))
        if name == "Z":
            arrived(r.oz_r.at[index[0]], r.om.at[x, y, index[0], half])
        elif name == "X":
            k, g = index
            a, b = X_GROUPS[g]
            arrived(r.ox_r.at[k, g], r.om.at[slab_x(1 + k), y, a:b, half])
        elif name == "Y":
            xi, g = index
            a, b = Y_GROUPS[g]
            arrived(r.oy_r.at[xi, g], r.om.at[slab_x(xi), 1 - y, a:b, half])
        else:
            yi, xi = index
            arrived(r.ob_r.at[yi, xi], r.om.at[slab_x(xi), y if yi == 0 else 1 - y, :, half])

    def slab_x(xi):
        return (x + (0, -d, d, 2)[xi] + 4) % 4

    def need_slab(xi, first, last):
        if xi == 0:
            for k in range(max(first, 1), last):
                need("Z", k)
        else:
            for g, (a, b) in enumerate(X_GROUPS):
                if a < last and b > first:
                    need("X", xi - 1, g)

    def z_send(oz):
        k = OFFSETS.index(-oz % NZ)
        send(r.om.at[x, y, 0, half], r.om.at[x, y, k, half], r.oz_s, r.oz_r.at[k], to(x, y, z + oz))

    def z_pass():
        need("Z", 5)
        need("Z", 6)
        send(r.om.at[x, y, 6 - c, half], r.om.at[x, y, 7, half], r.oz_s, r.oz_r.at[7], to(x, y, z + d))

    def x_send(g, k):
        a, b = X_GROUPS[g]
        need_slab(1 if k == 2 else 0, a, b)
        piece = r.om.at[slab_x(1 if k == 2 else 0), y, a:b, half]
        send(piece, piece, r.ox_s, r.ox_r.at[k, g], to(x - d if k == 1 else x + d, y, z))

    def y_send(xi, g):
        a, b = Y_GROUPS[g]
        need_slab(xi, a, b)
        for side, device in enumerate((to(x, 1 - y, z), across)):
            piece = r.om.at[slab_x(xi), y, a:b, 2 * c + side]
            send(piece, piece, r.oy_s, r.oy_r.at[xi, g], device)

    def share(xi, yi):
        if yi == 0:
            need_slab(xi, 0, NZ)
        else:
            for g in range(len(Y_GROUPS)):
                need("Y", xi, g)
        piece = r.om.at[slab_x(xi), y if yi == 0 else 1 - y, :, half]
        send(piece, piece, r.ob_s, r.ob_r.at[yi, (0, 2, 1, 3)[xi]], sibling)

    terms = []

    def sketch(xi, yi):
        if not terms:
            copy_a.wait()
        need("B", yi, xi)
        xx, yy = slab_x(xi), y if yi == 0 else 1 - y
        columns = [r.a[:, pl.ds(pl.multiple_of(at(xx, yy, z + o) * 128, 128), 128)] for o in OFFSETS]
        omega = r.om[xx, yy].reshape(1024, 256)
        value = jnp.dot(jnp.concatenate(columns, axis=1), omega, preferred_element_type=F32)
        r.acc[...] = r.acc[...] + value if terms else value
        terms.append((xi, yi))

    gather = dict(z=z_send, zp=z_pass, x=x_send, y=y_send, s=share, k=sketch)
    for name, *args in GATHER:
        gather[name](*args)

    for s in range(2):
        r.st[s] = r.acc[256 * s : 256 * s + 256].astype(BF16).astype(F32).T.astype(BF16)

    def term(pieces, block, received, out):
        columns = pl.ds(pl.multiple_of(block * 128, 128), 128)
        row = 0
        for s, k0, k1 in pieces:
            n = k1 - k0
            value = jnp.dot(r.st[s, k0:k1, :], r.a[256 * s : 256 * s + 256, columns], preferred_element_type=F32)
            for ref in received:
                value = value + ref[row : row + n, :].astype(F32)
            out[row : row + n, :] = value.astype(out.dtype)
            row += n

    def sg(way):
        return 1 - 2 * way

    def z_off(q):
        return 4 + (q // 2) * (1 - q % 2) - ((q + 1) // 2) * (q % 2)

    def x_off(q):
        return 2 - q + 3 * (q // 2) + 2 * (q // 3)

    def x_send_on(way, s, q):
        if s == 0:
            src, dst = r.xs.at[way, 0, q, way], r.xr.at[way, 0, q, way]
        else:
            src, dst = r.xs.at[way, 1, q], r.xr.at[way, 1, q]
        send(src, dst, r.x_s.at[s], r.x_r.at[s, q], to(x + sg(way), y, z))

    def x1(q):
        for way in (0, 1):
            term(X_PIECES, at(x + 2, way, z + z_off(q)), [], r.xs.at[way, 0, q, way])
            x_send_on(way, 0, q)

    def x2(q):
        arrived(r.x_r.at[0, q], r.xr.at[0, 0, q])
        for way in (0, 1):
            for yy in (0, 1):
                got = [r.xr.at[way, 0, q, way]] if yy == way else []
                term(X_PIECES, at(x + sg(way), yy, z + z_off(q)), got, r.xs.at[way, 1, q, yy])
            x_send_on(way, 1, q)

    def x_fin(q):
        arrived(r.x_r.at[1, q], r.xr.at[:, 1, q])
        for yy in (0, 1):
            got = [r.xr.at[way, 1, q, yy] for way in (0, 1)]
            term(X_PIECES, at(x, yy, z + z_off(q)), got, r.xacc.at[q, yy])
        r.xys[q] = r.xacc[q, 1 - y].astype(BF16)
        send(r.xys.at[q], r.xy.at[q], r.xy_s, r.xy_r.at[q], to(x, 1 - y, z))

    def halves(way, rows):
        return pl.ds(way * (rows // 2), rows // 2)

    def ring_step(total, sent, received, send_sem, recv_sem, s, rows, devices):
        if s:
            ring_arrived(received, recv_sem, s - 1)
        else:
            farthest = total(0)
        for way in (0, 1):
            half_rows = halves(way, rows)
            if s == 0:
                sent[way, 0, half_rows] = farthest[way * (rows // 2) : (way + 1) * (rows // 2)]
                src, dst = sent.at[way, 0, half_rows], received.at[way, 0, half_rows]
            else:
                sent[way, s] = total(2 * s - 1 + way)
                part = half_rows if s == 1 else pl.ds(0, rows)
                sent[way, s, part] += received[way, s - 1, part]
                src, dst = sent.at[way, s], received.at[way, s]
            send(src, dst, send_sem.at[min(s, 1)], recv_sem.at[s], devices[way])

    def ring_arrived(received, recv_sem, s):
        arrived(recv_sem.at[s], received.at[0, 0] if s == 0 else received.at[:, s])

    def x_total(q):
        arrived(r.xy_r.at[q], r.xy.at[q])
        return r.xacc[q, y] + r.xy[q].astype(F32)

    def xz(s):
        ring_step(x_total, r.xzs, r.xzr, r.xz_s, r.xz_r, s, KX, (to(x, y, z + 1), to(x, y, z - 1)))

    def z_arrived(s, q):
        arrived(r.z_r.at[s, q], r.zr.at[0, 0, q] if s == 0 else r.zr.at[:, s, q])

    def z_step(s, q):
        if s:
            z_arrived(s - 1, q)
        for way in (0, 1):
            far = z + sg(way) * (4 - s)
            if s == 0:
                term(Z_PIECES, at(x + x_off(q), way, far), [], r.zs.at[way, 0, q, way])
                src, dst = r.zs.at[way, 0, q, way], r.zr.at[way, 0, q, way]
            else:
                for yy in (0, 1):
                    got = [r.zr.at[way, s - 1, q, yy]] if s > 1 or yy == way else []
                    term(Z_PIECES, at(x + x_off(q), yy, far), got, r.zs.at[way, s, q, yy])
                src, dst = r.zs.at[way, s, q], r.zr.at[way, s, q]
            send(src, dst, r.z_s.at[min(s, 1)], r.z_r.at[s, q], to(x, y, z + sg(way)))

    def z_fin(q):
        z_arrived(3, q)
        for yy in (0, 1):
            got = [r.zr.at[way, 3, q, yy] for way in (0, 1)]
            term(Z_PIECES, at(x + x_off(q), yy, z), got, r.zacc.at[q, yy])
        send(r.zacc.at[q, 1 - y], r.zy.at[q], r.zy_s, r.zy_r.at[q], to(x, 1 - y, z))

    def z_total(q):
        arrived(r.zy_r.at[q], r.zy.at[q])
        return r.zacc[q, y] + r.zy[q]

    def zx(s):
        ring_step(z_total, r.zxs, r.zxr, r.zx_s, r.zx_r, s, KZ, (to(x + 1, y, z), to(x - 1, y, z)))

    def g_local():
        for s in range(2):
            value = jnp.dot(r.st[s], r.acc[256 * s : 256 * s + 256].astype(BF16), preferred_element_type=F32)
            r.gl[s] = value.reshape(4, 8, 8, 256)
        for o in (1, 2, 3, 0):
            k = (x + o) % 4
            send(r.gl.at[1 - y, k], r.gy.at[k], r.gy_s, r.gy_r.at[o], to(x, 1 - y, z))

    def g_x(o):
        k = (x + o) % 4
        arrived(r.gy_r.at[o], r.gy.at[k])
        r.gy[k] += r.gl[y, k]
        if o:
            send(r.gy.at[k], r.gx.at[o - 1], r.gx_s, r.gx_r, to(x + o, y, z))

    def g_z():
        arrived(r.gx_r, r.gx)
        r.gs[...] = r.gy[x] + r.gx[0] + r.gx[1] + r.gx[2]
        for o in range(1, NZ):
            send(r.gs.at[(z + o) % 8], r.gz.at[o - 1], r.gz_s, r.gz_r, to(x, y, z + o))

    def h_z():
        arrived(r.gz_r, r.gz)
        total = r.gs[z]
        for o in range(1, NZ):
            total = total + r.gz[o - 1]
        r.gf[x, z] = total
        piece = r.gf.at[x, z]
        for o in range(1, NZ):
            send(piece, piece, r.hz_s, r.hz_r, to(x, y, z + o))

    def h_x():
        arrived(r.hz_r, r.gf.at[x, 0:7])
        piece = r.gf.at[x]
        for o in range(1, NX):
            send(piece, piece, r.hx_s, r.hx_r, to(x + o, y, z))

    def c_start():
        arrived(r.hx_r, r.gf.at[0:3])
        r.m[:, :256] = r.gf[...].reshape(256, 256)
        row = lax.broadcasted_iota(jnp.int32, (256, 256), 0)
        column = lax.broadcasted_iota(jnp.int32, (256, 256), 1)
        r.m[:, 256:] = jnp.where(row == column, 1.0, 0.0).astype(F32)

    def c_group(b):
        factor_group(r.m, b)
        if (8 * b + 8) % PANEL == 0:
            p = 8 * b // PANEL
            trailing(r.m, p)
            rows = slice(PANEL * p, PANEL * p + PANEL)
            send(r.m.at[rows, 256:512], r.li.at[rows], r.l_s, r.l_r, to(x, 1 - y, z))

    groups = iter(range(32))

    def c_next(n):
        for b in [b for _, b in zip(range(n), groups)]:
            c_group(b)

    steps = dict(
        gl=g_local, z=z_step, x1=x1, x2=x2, gx=g_x, gz=g_z, hz=h_z, hx=h_x, xf=x_fin, zf=z_fin, xz=xz, zx=zx, cs=c_start, c=c_next
    )
    for name, *args in SCHEDULE:
        steps[name](*args)

    for pieces, total, last, received, recv_sem, ring in (
        (Z_PIECES, z_total, 3, r.zxr, r.zx_r, 2),
        (X_PIECES, x_total, 7, r.xzr, r.xz_r, 4),
    ):
        value = total(last)
        ring_arrived(received, recv_sem, ring - 1)
        value = value + received[0, ring - 1] + received[1, ring - 1]
        row = 0
        for s, k0, k1 in pieces:
            n = k1 - k0
            r.pt[s, k0:k1, :] = value[row : row + n]
            row += n

    def solved(s, inverse):
        return lax.dot_general(
            r.pt[s], inverse, (((0,), (1,)), ((), ())), precision=HI, preferred_element_type=F32
        )

    mine = solved(y, r.m[:, 256:])
    arrived(r.l_r, r.li)
    others = solved(1 - y, r.li[...])
    out[:, 0, :] = jnp.where(y == 0, mine, others)
    out[:, 1, :] = jnp.where(y == 0, others, mine)

    for sem, ref in (
        (r.oz_s, r.om.at[x, y, 0:7, half]),
        (r.ox_s, r.om.at[0:3, 0, :, half]),
        (r.oy_s, r.om.at[:, 0, :, half]),
        (r.ob_s, r.om.at[:, :, :, half]),
        (r.x_s.at[0], r.xs.at[0, 0]),
        (r.x_s.at[1], r.xs.at[:, 1]),
        (r.xy_s, r.xys),
        (r.xz_s.at[0], r.xzs.at[0, 0]),
        (r.xz_s.at[1], r.xzs.at[:, 1:4]),
        (r.z_s.at[0], r.zs.at[0, 0]),
        (r.z_s.at[1], r.zs.at[:, 1:4]),
        (r.zy_s, r.zacc.at[:, 0]),
        (r.zx_s.at[0], r.zxs.at[0, 0]),
        (r.zx_s.at[1], r.zxs.at[:, 1]),
        (r.gy_s, r.gl.at[0]),
        (r.gx_s, r.gx),
        (r.gz_s, r.gz),
        (r.hz_s, r.gz),
        (r.hx_s, r.gx),
        (r.l_s, r.li),
    ):
        arrived(sem, ref)


def local(panels, test_matrix):
    return pl.pallas_call(
        kernel,
        out_shape=jax.ShapeDtypeStruct((128, 2, 256), F32),
        in_specs=[pl.BlockSpec(memory_space=pl.ANY), pl.BlockSpec(memory_space=pltpu.VMEM)],
        out_specs=pl.BlockSpec(memory_space=pltpu.VMEM),
        scratch_shapes=SHAPES,
        compiler_params=pltpu.CompilerParams(
            collective_id=0, has_side_effects=True, vmem_limit_bytes=60 * 1024 * 1024
        ),
    )(panels.reshape(512, 8192), test_matrix.reshape(4, 32, 256))


def solution(mesh):
    in_specs = (P("freq", None, "blk", None), P("blk", None))
    out_specs = P("blk", "freq", None)
    return jax.shard_map(local, mesh=mesh, in_specs=in_specs, out_specs=out_specs, check_vma=False)
```
